256 devices in a mesh: grp: 2 (over core), beam: 8 (over z_lo, y), row: 16 (over x, z_hi).
Axes of the slice: x: 4, y: 4, z: 8 (z_hi: 4, z_lo: 2; z = z_hi * 2 + z_lo), core: 2. Of those that a mesh axis runs over, the one named last changes fastest.
Arguments:
- densities: bfloat16 [32, 256, 32, 2048], P(None, 'grp', 'beam', 'row'), may hold values from 0 to 1
- spectra: bfloat16 [256, 2048, 512], P(('grp', 'beam'), 'row'), may hold values from -6 to 6
- intensities: bfloat16 [8192, 4096], P(('grp', 'beam', 'row')), may hold values from 0.099609375 to 4
- positions: int32 [8192, 2], P(('grp', 'beam', 'row')), may hold values from 0 to 64, as said below
- probe: float32 [2, 4096], replicated, may hold values from -6 to 6
- line_channels: int32 [32, 4], replicated, may hold values from 0 to 511
- line_weights: float32 [32, 4], replicated, may hold values from 0.2 to 1
- atten_coef: float32 [32], replicated, may hold values from 0.00048828125 to 0.00390625
- beta_coef: float32 [32], replicated, may hold values from 0.0001953125 to 0.001953125
- delta_coef: float32 [32], replicated, may hold values from 0.0009765625 to 0.0078125
Outputs:
- density_grad: bfloat16 [32, 256, 32, 2048], P(None, 'grp', 'beam', 'row')
- probe_grad: float32 [2, 4096], replicated
The draws below stay inside these ranges and needn't reach their ends.
Inputs may be any that keep to these rules, and one draw needn't show every extreme that they name: `positions`: column 0 is within 0 to 64, column 1 within 0 to 64; each device's first position has the largest layer offset and its second the largest row offset.
All inputs are finite; a program needn't handle non-finite values.
Results may differ from the reference program's by a relative error of at most 0.001.
Values sent between devices are 32-bit elements; how exact they have to be, the bound alone decides.
A program may use at most 128 MiB of HBM per device.

```python
import math
import jax
import jax.numpy as jnp
from jax import lax

E = 32
C = 512
LINES = 4
M = 64
ZD = 128
YD = 128
K = 32
NZ = 256
NX = 32
NY = 2048
TOTALPOS = 8192
N_BEAM = 8
N_ROW = 16


def draw_positions(key, part):
    key = jax.random.fold_in(key, 11)
    first_key, second_key = jax.random.split(key)
    along_z = jax.random.randint(first_key, (TOTALPOS,), 0, ZD - M + 1)
    along_y = jax.random.randint(second_key, (TOTALPOS,), 0, YD - M + 1)
    along_z = along_z.at[::K].set(ZD - M)
    along_y = along_y.at[1::K].set(YD - M)
    return jnp.stack([along_z, along_y], axis=1).astype(jnp.int32)


def set_ends(entries, stream_key, least, largest):
    longest = entries.shape.index(max(entries.shape))
    spots = []
    for shift in (0, 1):
        where = [jax.random.randint(jax.random.fold_in(stream_key, axis), (), 0, length) for axis, length in enumerate(entries.shape)]
        where[longest] = (where[longest] + shift) % entries.shape[longest]
        spots.append(tuple(where))
    return entries.at[spots[0]].set(least).at[spots[1]].set(largest)


def level_of(own_key, extent, pieces, low, high):
    level = 1.0
    for axis_at, parts in pieces:
        heights = jax.random.uniform(jax.random.fold_in(jax.random.fold_in(own_key, 6), axis_at), (parts,), jnp.float32, low / len(pieces), high / len(pieces))
        level = level * jnp.repeat(jnp.exp(heights), extent[axis_at] // parts).reshape((-1,) + (1,) * (len(extent) - 1 - axis_at))
    return level


def normal_values(stream_key, shape, deviation, bound, cuts=(), held_as=jnp.bfloat16):
    factor_of = level_of(stream_key, shape, cuts, -0.22, 0.18) if cuts else 1.0
    entries = jax.random.normal(stream_key, shape, jnp.float32) * deviation * factor_of
    return jnp.minimum(jnp.maximum(entries, -bound), bound).astype(held_as)


def setup_inputs(seed: int = 0) -> dict:
    seeds = jax.random.split(jax.random.key(seed), 11)
    return {
        "densities": jnp.clip(1.0 * jax.random.uniform(seeds[0], (E, NZ, NX, NY), jnp.float32) ** level_of(seeds[0], (E, NZ, NX, NY), ((1, 2), (2, 8), (3, 16)), -0.2, 0.2), 0.0, 1.0).astype(jnp.bfloat16),
        "spectra": normal_values(seeds[1], (NZ, NY, C), 1.0, 6.0, ((0, 16), (1, 16))),
        "intensities": jnp.clip(jnp.exp(math.log(4.0) - 3.6927934 * jax.random.uniform(seeds[2], (TOTALPOS, M * M), jnp.float32) ** level_of(seeds[2], (TOTALPOS, M * M), ((0, 256),), -0.2, 0.2)), 0.099609375, 4.0).astype(jnp.bfloat16),
        "positions": draw_positions(jax.random.fold_in(seeds[10], 71), 0),
        "probe": normal_values(seeds[4], (2, M * M), 1.0, 6.0, (), jnp.float32),
        "line_channels": set_ends(jax.random.randint(seeds[5], (E, LINES), 0, C), jax.random.fold_in(seeds[5], 1), 0, C - 1).astype(jnp.int32),
        "line_weights": jnp.clip(jnp.exp(jax.random.uniform(seeds[6], (E, LINES), jnp.float32, math.log(0.2), math.log(1.0))), 0.2, 1.0),
        "atten_coef": jnp.clip(jnp.exp(jax.random.uniform(seeds[7], (E,), jnp.float32, math.log(0.00048828125), math.log(0.00390625))), 0.00048828125, 0.00390625),
        "beta_coef": jnp.clip(jnp.exp(jax.random.uniform(seeds[8], (E,), jnp.float32, math.log(0.0001953125), math.log(0.001953125))), 0.0001953125, 0.001953125),
        "delta_coef": jnp.clip(jnp.exp(jax.random.uniform(seeds[9], (E,), jnp.float32, math.log(0.0009765625), math.log(0.0078125))), 0.0009765625, 0.0078125),
    }


HIGHEST = lax.Precision.HIGHEST
object_weight = 1000.0

def line_table(line_channels, line_weights, channels):
    grid = jnp.arange(channels, dtype=jnp.float32)
    offset = grid[None, None, :] - line_channels.astype(jnp.float32)[:, :, None]
    shapes = line_weights[:, :, None] * jnp.exp(-offset * offset / 8.0)
    return lax.optimization_barrier(jnp.sum(shapes, axis=1))

def dft_tables(points):
    index = jnp.arange(points, dtype=jnp.int32)
    product = index[:, None] * index[None, :] % points
    angles = 2.0 * math.pi / points * product.astype(jnp.float32)
    factor = 1.0 / math.sqrt(points)
    return (jnp.cos(angles) * factor, -jnp.sin(angles) * factor)

def chirp_tables(points):
    centred = jnp.arange(points, dtype=jnp.float32) - float(points // 2)
    angles = math.pi * 0.5 / points * (centred[:, None] * centred[:, None] + centred[None, :] * centred[None, :])
    return (jnp.cos(angles), jnp.sin(angles))

def complex_mul(left_real, left_imag, right_real, right_imag):
    return (left_real * right_real - left_imag * right_imag, left_real * right_imag + left_imag * right_real)

def apply_table(values_real, values_imag, table_real, table_imag):
    first_real = jnp.einsum('ab,kbc->kac', table_real, values_real, precision=HIGHEST) - jnp.einsum('ab,kbc->kac', table_imag, values_imag, precision=HIGHEST)
    first_imag = jnp.einsum('ab,kbc->kac', table_real, values_imag, precision=HIGHEST) + jnp.einsum('ab,kbc->kac', table_imag, values_real, precision=HIGHEST)
    out_real = jnp.einsum('kac,cd->kad', first_real, table_real, precision=HIGHEST) - jnp.einsum('kac,cd->kad', first_imag, table_imag, precision=HIGHEST)
    out_imag = jnp.einsum('kac,cd->kad', first_real, table_imag, precision=HIGHEST) + jnp.einsum('kac,cd->kad', first_imag, table_real, precision=HIGHEST)
    return (out_real, out_imag)

def ptycho_terms(win_real, win_imag, probe_real, probe_imag, measured, points):
    table_real, table_imag = dft_tables(points)
    chirp_real, chirp_imag = chirp_tables(points)
    exit_real, exit_imag = complex_mul(probe_real[None], probe_imag[None], win_real, win_imag)
    exit_real, exit_imag = complex_mul(exit_real, exit_imag, chirp_real[None], chirp_imag[None])
    far_real, far_imag = apply_table(exit_real, exit_imag, table_real, table_imag)
    misfit = far_real * far_real + far_imag * far_imag - measured.astype(jnp.float32).reshape(-1, points, points)
    back_real, back_imag = apply_table(misfit * far_real, misfit * far_imag, table_real, -table_imag)
    back_real, back_imag = complex_mul(back_real, back_imag, chirp_real[None], -chirp_imag[None])
    grad_real, grad_imag = complex_mul(probe_real[None], -probe_imag[None], back_real, back_imag)
    probe_real_sum, probe_imag_sum = complex_mul(win_real, -win_imag, back_real, back_imag)
    return (grad_real, grad_imag, lax.optimization_barrier(jnp.sum(probe_real_sum, axis=0)), lax.optimization_barrier(jnp.sum(probe_imag_sum, axis=0)))

def reference(densities, spectra, intensities, positions, probe, line_channels, line_weights, atten_coef, beta_coef, delta_coef):
    table = line_table(line_channels, line_weights, C)

    def forward_layer(layer):
        density = lax.dynamic_index_in_dim(densities, layer, 1, keepdims=False).astype(jnp.float32)
        optical = jnp.einsum('exy,e->xy', density, atten_coef, precision=HIGHEST)
        incident = jnp.exp(-(jnp.cumsum(optical, axis=0) - optical))
        emitted = jnp.einsum('exy,xy->ey', density, incident, precision=HIGHEST)
        absorb = jnp.einsum('exy,e->y', density, beta_coef, precision=HIGHEST)
        phase = jnp.einsum('exy,e->y', density, delta_coef, precision=HIGHEST)
        fitted = jnp.einsum('ey,ec->yc', emitted, table, precision=HIGHEST)
        residual = fitted - lax.dynamic_index_in_dim(spectra, layer, 0, keepdims=False).astype(jnp.float32)
        element_grad = jnp.einsum('yc,ec->ey', residual, table, precision=HIGHEST)
        return (absorb, phase, element_grad)
    absorb, phase, element_grad = lax.map(forward_layer, jnp.arange(NZ, dtype=jnp.int32))
    amplitude = jnp.exp(-absorb)
    obj_real = amplitude * jnp.cos(phase)
    obj_imag = amplitude * jnp.sin(phase)
    probe_real = probe[0].reshape(M, M)
    probe_imag = probe[1].reshape(M, M)

    def cut_window(field, start_z, start_y):
        return lax.dynamic_slice(field, (start_z, start_y), (M, M))

    def batch_step(carry, device):
        acc_real, acc_imag, sum_real, sum_imag = carry
        block = lax.dynamic_slice_in_dim(positions, device * K, K, 0)
        measured = lax.dynamic_slice_in_dim(intensities, device * K, K, 0)
        grp_index = device // (N_BEAM * N_ROW)
        row_index = device % N_ROW
        starts_z = (grp_index * ZD + block[:, 0]).astype(jnp.int32)
        starts_y = (row_index * YD + block[:, 1]).astype(jnp.int32)
        win_real = jax.vmap(cut_window, in_axes=(None, 0, 0))(obj_real, starts_z, starts_y)
        win_imag = jax.vmap(cut_window, in_axes=(None, 0, 0))(obj_imag, starts_z, starts_y)
        grad_real, grad_imag, probe_real_sum, probe_imag_sum = ptycho_terms(win_real, win_imag, probe_real, probe_imag, measured, M)

        def add_window(index, pair):
            field_real, field_imag = pair
            corner = (starts_z[index], starts_y[index])
            field_real = lax.dynamic_update_slice(field_real, lax.dynamic_slice(field_real, corner, (M, M)) + grad_real[index], corner)
            field_imag = lax.dynamic_update_slice(field_imag, lax.dynamic_slice(field_imag, corner, (M, M)) + grad_imag[index], corner)
            return (field_real, field_imag)
        acc_real, acc_imag = lax.fori_loop(0, K, add_window, (acc_real, acc_imag))
        return ((acc_real, acc_imag, sum_real + probe_real_sum, sum_imag + probe_imag_sum), None)
    zero_field = jnp.zeros((NZ, NY), jnp.float32)
    zero_probe = jnp.zeros((M, M), jnp.float32)
    carry, unused = lax.scan(batch_step, (zero_field, zero_field, zero_probe, zero_probe), jnp.arange(TOTALPOS // K, dtype=jnp.int32))
    tile_real, tile_imag, sum_real, sum_imag = carry
    probe_grad = jnp.stack([sum_real.reshape(M * M), sum_imag.reshape(M * M)]) / float(TOTALPOS)
    grad_absorb = -object_weight * (obj_real * tile_real + obj_imag * tile_imag)
    grad_phase = object_weight * (obj_real * tile_imag - obj_imag * tile_real)

    def gradient_layer(layer):
        density = lax.dynamic_index_in_dim(densities, layer, 1, keepdims=False).astype(jnp.float32)
        optical = jnp.einsum('exy,e->xy', density, atten_coef, precision=HIGHEST)
        incident = jnp.exp(-(jnp.cumsum(optical, axis=0) - optical))
        layer_grad = element_grad[layer]
        weighted = jnp.einsum('ey,exy->xy', layer_grad, density, precision=HIGHEST) * incident
        beyond = lax.optimization_barrier(jnp.sum(weighted, axis=0))[None, :] - jnp.cumsum(weighted, axis=0)
        result = layer_grad[:, None, :] * incident[None] - atten_coef[:, None, None] * beyond[None]
        result = result + beta_coef[:, None, None] * grad_absorb[layer][None, None, :] + delta_coef[:, None, None] * grad_phase[layer][None, None, :]
        return result.astype(jnp.bfloat16)
    stacked = lax.map(gradient_layer, jnp.arange(NZ, dtype=jnp.int32))
    return (jnp.moveaxis(stacked, 0, 1), probe_grad)
```

```python
import functools
import math

import jax
import jax.numpy as jnp
import numpy as np
from jax import lax
from jax.experimental import pallas as pl
from jax.experimental.pallas import tpu as pltpu
from jax.sharding import PartitionSpec as P

E = 32
C = 512
M = 64
K = 32
X = 4
ZB = 16
NB = 8
GROUP = 16

F32 = jnp.float32
BF16 = jnp.bfloat16
HIGHEST = lax.Precision.HIGHEST
MESH = pl.DeviceIdType.MESH
object_weight = 1000.0


def halves(values):
    high = values.astype(BF16)
    return high, (values - high.astype(F32)).astype(BF16)


def swap(values):
    return pltpu.roll(values, M, 1)


def matmul(left, right):
    return jnp.dot(left, right, preferred_element_type=F32)


def np_halves(values):
    high = values.astype(np.float32).astype(jnp.bfloat16)
    low = (values - high.astype(np.float64)).astype(np.float32).astype(jnp.bfloat16)
    return high, low


def constant_tables():
    index = np.arange(M)
    angles = 2.0 * math.pi / M * (index[:, None] * index[None, :] % M)
    dft_real = np.cos(angles) / math.sqrt(M)
    dft_imag = -np.sin(angles) / math.sqrt(M)
    centred = np.arange(M) - M // 2
    chirp = math.pi * 0.5 / M * (centred[:, None] ** 2 + centred[None, :] ** 2)
    chirp_real, chirp_imag = np.cos(chirp), np.sin(chirp)
    chirps = np.stack(
        [
            np.concatenate([chirp_real, chirp_real], 1),
            np.concatenate([-chirp_imag, chirp_imag], 1),
        ]
    ).astype(np.float32)

    def right_table(sign):
        table = np.block([[dft_real, sign * dft_imag], [-sign * dft_imag, dft_real]])
        high, low = np_halves(table)
        row = np.concatenate([high, low], 1)
        return np.concatenate([row, row], 0)

    right = np.stack([right_table(1.0), right_table(-1.0)])
    high, low = np_halves(np.concatenate([dft_real, dft_imag], 0))
    left = np.concatenate([high, high, low, low], 1)
    return chirps, right, left


def kernel(
    sizes,
    dens_hbm,
    spec_hbm,
    inten_ref,
    pos_ref,
    probe_ref,
    chan_ref,
    weight_ref,
    atten_ref,
    beta_ref,
    delta_ref,
    chirp_ref,
    right_ref,
    left_ref,
    out_hbm,
    probe_out,
    dens_bf,
    dens_f,
    spec_v,
    tap_src,
    tap_rcv,
    u_src,
    u_rcv,
    ow_src,
    ow_rcv,
    inc_ref,
    tg_src,
    tg_rcv,
    lg_src,
    lg_rcv,
    eg_ref,
    mix_ref,
    fit_ref,
    out_v,
    tile_ref,
    pgsum_ref,
    pr_src,
    pr_rcv,
    pa_rcv,
    pb_rcv,
    pf_rcv,
    dens_sem,
    spec_sem,
    out_sem,
    tap_ss,
    tap_rs,
    u_ss,
    u_rs,
    ow_ss,
    ow_rs,
    tg_ss,
    tg_rs,
    lg_ss,
    lg_rs,
    eg_ss,
    eg_rs,
    pr_ss,
    pr_rs,
    pa_ss,
    pa_rs,
    pb_ss,
    pb_rs,
    pf_ss,
    pf_rs,
):
    n_grp, n_row, n_x, n_zh, total = sizes
    me = lax.axis_index("beam")
    grp = lax.axis_index("grp")
    row = lax.axis_index("row")
    row_x, row_z = row // n_zh, row % n_zh
    n_near = n_grp * n_zh
    near = grp * n_zh + row_z

    def near_id(step):
        other = (near + step) % n_near
        return {"grp": other // n_zh, "row": row_x * n_zh + other % n_zh}

    def x_id(step):
        return {"row": ((row_x + step) % n_x) * n_zh + row_z}

    def peer(step):
        return (me + step) % NB

    def remote(source, target, send, recv, device):
        return pltpu.make_async_remote_copy(
            src_ref=source,
            dst_ref=target,
            send_sem=send,
            recv_sem=recv,
            device_id=device,
            device_id_type=MESH,
        )

    barrier = pltpu.get_barrier_semaphore()
    for step in range(1, NB):
        pl.semaphore_signal(barrier, inc=1, device_id={"beam": peer(step)}, device_id_type=MESH)
    for step in range(1, n_near):
        pl.semaphore_signal(barrier, inc=1, device_id=near_id(step), device_id_type=MESH)
    for step in range(1, n_x):
        pl.semaphore_signal(barrier, inc=1, device_id=x_id(step), device_id_type=MESH)

    def dens_copy(step):
        block = (me + 1 + step) % NB
        return pltpu.make_async_copy(
            dens_hbm.at[:, block], dens_bf.at[:, block], dens_sem.at[step]
        )

    for step in range(NB):
        dens_copy(step).start()
    spec_copy = pltpu.make_async_copy(spec_hbm, spec_v, spec_sem)
    spec_copy.start()

    channel = lax.broadcasted_iota(jnp.int32, (E, C), 1).astype(F32)
    table = jnp.zeros((E, C), F32)
    for line in range(4):
        offset = channel - chan_ref[:, line : line + 1]
        table = table + weight_ref[:, line : line + 1] * jnp.exp(-offset * offset / 8.0)
    gram = lax.dot_general(
        table, table, (((1,), (1,)), ((), ())), precision=HIGHEST, preferred_element_type=F32
    )

    pl.semaphore_wait(barrier, NB - 1 + n_near - 1 + n_x - 1)

    def cell(e, block, x):
        return dens_f[e, block, pl.ds(x, ZB, stride=X), :]

    def project(step, carry):
        block = (me + 1 + step) % NB
        dens_copy(step).wait()
        dens_f[:, block] = dens_bf[:, block].astype(F32)

        def add(e, sums):
            cells = [cell(e, block, x) for x in range(X)]
            total_cells = (cells[0] + cells[1]) + (cells[2] + cells[3])
            optical = [sums[x] + atten_ref[e] * cells[x] for x in range(X)]
            return (
                *optical,
                sums[X] + beta_ref[e] * total_cells,
                sums[X + 1] + delta_ref[e] * total_cells,
            )

        zero = jnp.zeros((ZB, 128), F32)
        sums = lax.fori_loop(0, E, add, (zero,) * (X + 2), unroll=E)
        depth = zero
        for x in range(X):
            inc_ref[block, x] = jnp.exp(-depth)
            depth = depth + sums[x]
        tap_src[block, 0] = depth
        tap_src[block, 1] = sums[X]
        tap_src[block, 2] = sums[X + 1]

        @pl.when(step < NB - 1)
        def _():
            remote(
                tap_src.at[block],
                tap_rcv.at[me],
                tap_ss.at[step],
                tap_rs.at[me],
                {"beam": block},
            ).start()

        return carry

    lax.fori_loop(0, NB, project, 0)
    tap_rcv[me] = tap_src[me]

    def emit(step, carry):
        block = (me + 1 + step) % NB
        local = [inc_ref[block, x] for x in range(X)]

        def one(e, inner):
            terms = [cell(e, block, x) * local[x] for x in range(1, X)]
            u_src[block, e] = (cell(e, block, 0) + terms[0]) + (terms[1] + terms[2])
            return inner

        lax.fori_loop(0, E, one, 0, unroll=E)

        @pl.when(step < NB - 1)
        def _():
            remote(
                u_src.at[block], u_rcv.at[me], u_ss.at[step], u_rs.at[me], {"beam": block}
            ).start()

        return carry

    lax.fori_loop(0, NB, emit, 0)
    u_rcv[me] = u_src[me]

    for step in range(1, NB):
        src = peer(step)
        remote(tap_src.at[src], tap_rcv.at[src], tap_ss.at[0], tap_rs.at[src], {"beam": src}).wait_recv()
    before = jnp.zeros((ZB, 128), F32)
    absorb = jnp.zeros((ZB, 128), F32)
    phase = jnp.zeros((ZB, 128), F32)
    for d in range(NB):
        ow_src[d, 2] = jnp.exp(-before)
        before = before + tap_rcv[d, 0]
        absorb = absorb + tap_rcv[d, 1]
        phase = phase + tap_rcv[d, 2]
    amplitude = jnp.exp(-absorb)
    own_real = amplitude * jnp.cos(phase)
    own_imag = amplitude * jnp.sin(phase)
    for d in range(NB):
        ow_src[d, 0] = own_real
        ow_src[d, 1] = own_imag
    ow_sends = []
    for step in range(1, NB):
        dst = peer(step)
        copy = remote(
            ow_src.at[dst], ow_rcv.at[me], ow_ss.at[step], ow_rs.at[me], {"beam": dst}
        )
        copy.start()
        ow_sends.append(copy)
    ow_rcv[me] = ow_src[me]

    spec_copy.wait()
    table_high, table_low = halves(table)
    fit = lax.dot_general(
        jnp.concatenate([table_high, table_low], 0),
        spec_v[...],
        (((1,), (1,)), ((), ())),
        preferred_element_type=F32,
    )
    fit_ref[...] = fit[:E] + fit[E:]

    for step in range(1, NB):
        src = peer(step)
        remote(ow_src.at[src], ow_rcv.at[src], ow_ss.at[0], ow_rs.at[src], {"beam": src}).wait_recv()

    lane = lax.broadcasted_iota(jnp.int32, (M, 128), 1)
    first = lane < M
    probe = probe_ref[...]
    illum = probe * chirp_ref[0] + swap(probe) * chirp_ref[1]
    illum_swap = swap(illum)
    illum_a = jnp.where(first, illum, illum_swap)
    illum_b = jnp.where(first, -illum_swap, illum)
    sign = jnp.where(first, -1.0, 1.0).astype(F32)

    obj_real = ow_rcv[:, 0].reshape(NB * ZB, 128)
    obj_imag = ow_rcv[:, 1].reshape(NB * ZB, 128)
    real_high, real_low = halves(obj_real)
    imag_high, imag_low = halves(obj_imag)
    field = jnp.concatenate([real_high, imag_high, real_low, imag_low], 1)

    pick_z = lax.broadcasted_iota(jnp.int32, (M, 128), 1) - lax.broadcasted_iota(
        jnp.int32, (M, 128), 0
    )
    gather_row = lax.broadcasted_iota(jnp.int32, (256, 128), 0)
    gather_col = lax.broadcasted_iota(jnp.int32, (256, 128), 1)
    pick_y = jnp.where(
        (gather_row < 128) == (gather_col < M), gather_row % 128 - gather_col % M, -1
    )
    spread_row = lax.broadcasted_iota(jnp.int32, (128, 256), 0)
    spread_col = lax.broadcasted_iota(jnp.int32, (128, 256), 1)
    place_y = jnp.where(
        (spread_col < 128) == (spread_row < M), spread_col % 128 - spread_row % M, -1
    )
    place_z = lax.broadcasted_iota(jnp.int32, (128, 128), 0) - (
        lax.broadcasted_iota(jnp.int32, (128, 128), 1) % M
    )

    tile_ref[...] = jnp.zeros(tile_ref.shape, F32)
    pgsum_ref[...] = jnp.zeros(pgsum_ref.shape, F32)

    def transform(values, right, conj):
        high, low = halves(values)
        product = matmul(jnp.concatenate([high, low], 1), right)
        product = product[:, :128] + product[:, 128:]
        high, low = halves(product)
        outs = []
        for i in range(GROUP):
            part = slice(i * M, (i + 1) * M)
            stack = jnp.concatenate([high[part], low[part], high[part], low[part]], 0)
            both = matmul(left_ref[...], stack)
            turned = swap(both[M:]) * sign
            outs.append(both[:M] - turned if conj else both[:M] + turned)
        return outs

    def positions_step(group, carry):
        windows, picks = [], []
        starts = [
            (pos_ref[2 * (group * GROUP + i)], pos_ref[2 * (group * GROUP + i) + 1])
            for i in range(GROUP)
        ]
        for i in range(GROUP):
            rows = (pick_z == starts[i][0]).astype(F32).astype(BF16)
            cut = matmul(rows, field).astype(BF16)
            stack = jnp.concatenate([cut[:, :256], cut[:, 256:]], 0)
            columns = (pick_y == starts[i][1]).astype(F32).astype(BF16)
            both = matmul(stack, columns)
            windows.append(both[:M] + both[M:])
        exits = [w * illum_a + swap(w) * illum_b for w in windows]
        far = transform(jnp.concatenate(exits, 0), right_ref[0], False)
        pulled = []
        for i in range(GROUP):
            square = far[i] * far[i]
            start = pl.multiple_of((group * GROUP + i) * M, M)
            misfit = square + swap(square) - inten_ref[pl.ds(start, M), :].astype(F32)
            pulled.append(misfit * far[i])
        back = transform(jnp.concatenate(pulled, 0), right_ref[1], True)
        sum_a = pgsum_ref[0]
        sum_b = pgsum_ref[1]
        tile = tile_ref[...]
        for i in range(GROUP):
            sum_a = sum_a + windows[i] * back[i]
            sum_b = sum_b + swap(windows[i]) * back[i]
            grad = back[i] * illum_a - swap(back[i]) * illum_b
            high, low = halves(grad)
            columns = (place_y == starts[i][1]).astype(F32).astype(BF16)
            spread = matmul(jnp.concatenate([high, low], 0), columns).astype(BF16)
            rows = (place_z == starts[i][0]).astype(F32).astype(BF16)
            tile = tile + matmul(rows, spread)
        pgsum_ref[0] = sum_a
        pgsum_ref[1] = sum_b
        tile_ref[...] = tile
        return carry

    lax.fori_loop(0, K // GROUP, positions_step, 0)

    for d in range(NB):
        tg_src[d, 0] = tile_ref[d * ZB : (d + 1) * ZB, :128]
        tg_src[d, 1] = tile_ref[d * ZB : (d + 1) * ZB, 128:]
    sum_a, sum_b = pgsum_ref[0], pgsum_ref[1]
    conj_sum = jnp.where(first, sum_a + swap(sum_a), sum_b - swap(sum_b))
    local_probe = conj_sum * chirp_ref[0] - swap(conj_sum) * chirp_ref[1]
    for d in range(NB):
        pr_src[d] = local_probe[d * 8 : (d + 1) * 8]
    tg_sends, pr_sends = [], []
    for step in range(1, NB):
        dst = peer(step)
        copy = remote(
            tg_src.at[dst], tg_rcv.at[me], tg_ss.at[step], tg_rs.at[me], {"beam": dst}
        )
        copy.start()
        tg_sends.append(copy)
    for step in range(1, NB):
        dst = peer(step)
        copy = remote(
            pr_src.at[dst], pr_rcv.at[me], pr_ss.at[step], pr_rs.at[me], {"beam": dst}
        )
        copy.start()
        pr_sends.append(copy)
    tg_rcv[me] = tg_src[me]
    pr_rcv[me] = pr_src[me]

    def scale_block(block, carry):
        for x in range(X):
            inc_ref[block, x] = inc_ref[block, x] * ow_rcv[block, 2]
        return carry

    lax.fori_loop(0, NB, scale_block, 0)

    for step in range(1, NB):
        src = peer(step)
        remote(pr_src.at[src], pr_rcv.at[src], pr_ss.at[0], pr_rs.at[src], {"beam": src}).wait_recv()
    piece = pr_rcv[0]
    for d in range(1, NB):
        piece = piece + pr_rcv[d]
    pa_rcv[near] = piece
    pa_sends = []
    for step in range(1, n_near):
        copy = remote(
            pa_rcv.at[near], pa_rcv.at[near], pa_ss.at[step], pa_rs.at[near], near_id(step)
        )
        copy.start()
        pa_sends.append(copy)

    for step in range(1, NB):
        src = peer(step)
        remote(u_src.at[src], u_rcv.at[src], u_ss.at[0], u_rs.at[src], {"beam": src}).wait_recv()
    shield = [ow_src[d, 2] for d in range(NB)]

    def add_slabs(e, carry):
        value = u_rcv[0, e] * shield[0]
        for d in range(1, NB):
            value = value + u_rcv[d, e] * shield[d]
        mix_ref[pl.ds(e, ZB, stride=E), :] = value
        return carry

    lax.fori_loop(0, E, add_slabs, 0, unroll=4)
    columns = jnp.concatenate([mix_ref[z * E : (z + 1) * E, :] for z in range(ZB)], 1)
    grads = jnp.dot(gram, columns, precision=HIGHEST, preferred_element_type=F32) - fit_ref[...]
    for z in range(ZB):
        mix_ref[z * E : (z + 1) * E, :] = grads[:, z * 128 : (z + 1) * 128]

    def to_layers(e, carry):
        value = mix_ref[pl.ds(e, ZB, stride=E), :]
        eg_ref[me, 0, e] = value[:8]
        eg_ref[me, 1, e] = value[8:]
        return carry

    lax.fori_loop(0, E, to_layers, 0, unroll=4)

    beam_z, beam_y = me // 4, me % 4
    up = beam_z * 4 + (beam_y + 1) % 4
    down = beam_z * 4 + (beam_y + 3) % 4
    across = (1 - beam_z) * 4 + beam_y
    far_side = beam_z * 4 + (beam_y + 2) % 4
    across_up = (1 - beam_z) * 4 + (beam_y + 1) % 4
    across_down = (1 - beam_z) * 4 + (beam_y + 3) % 4
    across_far = (1 - beam_z) * 4 + (beam_y + 2) % 4

    eg_sends = []

    def hand(block, half, dst):
        copy = remote(
            eg_ref.at[block, half],
            eg_ref.at[block, half],
            eg_ss.at[len(eg_sends)],
            eg_rs.at[block, half],
            {"beam": dst},
        )
        copy.start()
        eg_sends.append(copy)

    def arrive(block, half):
        remote(
            eg_ref.at[block, half],
            eg_ref.at[block, half],
            eg_ss.at[0],
            eg_rs.at[block, half],
            {"beam": block},
        ).wait_recv()

    hand(me, 0, up)
    hand(me, 1, down)
    hand(me, 0, across)
    hand(me, 1, across)
    hand(me, 1, up)
    hand(me, 0, down)

    def weigh(e, sums):
        value = jnp.concatenate([eg_ref[me, 0, e], eg_ref[me, 1, e]], 0)
        return tuple(sums[d] + value * u_rcv[d, e] for d in range(NB))

    weighted = lax.fori_loop(0, E, weigh, (jnp.zeros((ZB, 128), F32),) * NB, unroll=4)

    for step in range(1, NB):
        src = peer(step)
        remote(tg_src.at[src], tg_rcv.at[src], tg_ss.at[0], tg_rs.at[src], {"beam": src}).wait_recv()
    tile_real = tg_rcv[0, 0]
    tile_imag = tg_rcv[0, 1]
    for d in range(1, NB):
        tile_real = tile_real + tg_rcv[d, 0]
        tile_imag = tile_imag + tg_rcv[d, 1]
    own_real, own_imag = ow_src[0, 0], ow_src[0, 1]
    grad_absorb = -object_weight * (own_real * tile_real + own_imag * tile_imag)
    grad_phase = object_weight * (own_real * tile_imag - own_imag * tile_real)
    later = jnp.zeros((ZB, 128), F32)
    for d in range(NB - 1, -1, -1):
        lg_src[d, 0] = later
        lg_src[d, 1] = grad_absorb
        lg_src[d, 2] = grad_phase
        later = later + weighted[d] * shield[d]
    lg_sends = []
    for step in range(1, NB):
        dst = peer(step)
        copy = remote(
            lg_src.at[dst], lg_rcv.at[me], lg_ss.at[step], lg_rs.at[me], {"beam": dst}
        )
        copy.start()
        lg_sends.append(copy)
    lg_rcv[me] = lg_src[me]

    def out_copy(order, block):
        start = pl.multiple_of(block * ZB, ZB)
        return pltpu.make_async_copy(
            out_v.at[:, :, pl.ds(start, ZB), :],
            out_hbm.at[:, :, pl.ds(start, ZB), :],
            out_sem.at[order],
        )

    def finish(order, block):
        start = pl.multiple_of(block * ZB, ZB)

        def grad_of(e):
            return jnp.concatenate([eg_ref[block, 0, e], eg_ref[block, 1, e]], 0)

        def weigh_cells(e, sums):
            value = grad_of(e)
            return tuple(sums[x] + value * cell(e, block, x) for x in range(X))

        zero = jnp.zeros((ZB, 128), F32)
        sums = lax.fori_loop(0, E, weigh_cells, (zero,) * X, unroll=E)
        light = [inc_ref[block, x] for x in range(X)]
        beyond = [None] * X
        running = lg_rcv[block, 0]
        for x in range(X - 1, -1, -1):
            beyond[x] = running
            running = running + light[x] * sums[x]
        absorb_grad, phase_grad = lg_rcv[block, 1], lg_rcv[block, 2]

        def write(e, carry):
            value = grad_of(e)
            shared = beta_ref[e] * absorb_grad + delta_ref[e] * phase_grad
            for x in range(X):
                result = value * light[x] - atten_ref[e] * beyond[x] + shared
                out_v[e, x, pl.ds(start, ZB), :] = result.astype(BF16)
            return carry

        lax.fori_loop(0, E, write, 0, unroll=E)
        out_copy(order, block).start()

    def extras(block):
        remote(lg_src.at[block], lg_rcv.at[block], lg_ss.at[0], lg_rs.at[block], {"beam": block}).wait_recv()

    arrive(down, 0)
    hand(down, 0, up)
    arrive(up, 1)
    hand(up, 1, down)
    arrive(across, 0)
    hand(across, 0, up)
    hand(across, 0, down)
    finish(0, me)
    arrive(across, 1)
    hand(across, 1, up)
    hand(across, 1, down)

    for step in range(1, n_near):
        src = (near + step) % n_near
        remote(pa_rcv.at[src], pa_rcv.at[src], pa_ss.at[0], pa_rs.at[src], near_id(step)).wait_recv()
    piece = pa_rcv[0]
    for d in range(1, n_near):
        piece = piece + pa_rcv[d]
    pb_rcv[row_x] = piece
    pb_sends = []
    for step in range(1, n_x):
        copy = remote(
            pb_rcv.at[row_x], pb_rcv.at[row_x], pb_ss.at[step], pb_rs.at[row_x], x_id(step)
        )
        copy.start()
        pb_sends.append(copy)

    arrive(down, 1)
    extras(down)
    finish(1, down)
    arrive(far_side, 0)
    hand(far_side, 0, across)
    arrive(far_side, 1)
    hand(far_side, 1, across)
    arrive(up, 0)
    extras(up)
    finish(2, up)
    extras(across)
    finish(3, across)

    for step in range(1, n_x):
        src = (row_x + step) % n_x
        remote(pb_rcv.at[src], pb_rcv.at[src], pb_ss.at[0], pb_rs.at[src], x_id(step)).wait_recv()
    piece = pb_rcv[0]
    for d in range(1, n_x):
        piece = piece + pb_rcv[d]
    pf_rcv[me] = piece * (1.0 / total)
    pf_sends = []
    for step in range(1, NB):
        copy = remote(
            pf_rcv.at[me], pf_rcv.at[me], pf_ss.at[step], pf_rs.at[me], {"beam": peer(step)}
        )
        copy.start()
        pf_sends.append(copy)

    extras(far_side)
    finish(4, far_side)
    arrive(across_up, 0)
    arrive(across_up, 1)
    extras(across_up)
    finish(5, across_up)
    arrive(across_down, 0)
    arrive(across_down, 1)
    extras(across_down)
    finish(6, across_down)
    for step in range(1, NB):
        src = peer(step)
        remote(pf_rcv.at[src], pf_rcv.at[src], pf_ss.at[0], pf_rs.at[src], {"beam": src}).wait_recv()
    for d in range(NB):
        probe_out[d * 8 : (d + 1) * 8, :] = pf_rcv[d]
    arrive(across_far, 0)
    arrive(across_far, 1)
    extras(across_far)
    finish(7, across_far)

    for step in range(NB - 1):
        block = (me + 1 + step) % NB
        remote(tap_src.at[block], tap_rcv.at[me], tap_ss.at[step], tap_rs.at[me], {"beam": block}).wait_send()
        remote(u_src.at[block], u_rcv.at[me], u_ss.at[step], u_rs.at[me], {"beam": block}).wait_send()
    for copy in ow_sends + tg_sends + pr_sends + pa_sends + eg_sends + lg_sends + pb_sends + pf_sends:
        copy.wait_send()
    for order, block in enumerate(
        [me, down, up, across, far_side, across_up, across_down, across_far]
    ):
        out_copy(order, block).wait()


def body(
    sizes,
    densities,
    spectra,
    intensities,
    positions,
    probe,
    line_channels,
    line_weights,
    atten_coef,
    beta_coef,
    delta_coef,
):
    n_grp, n_row, n_x, n_zh, total = sizes
    chirps, right, left = constant_tables()
    dens = densities.reshape(E, NB, ZB * X, 128)
    spec = spectra.reshape(ZB * 128, C)
    inten = intensities.reshape(K * M, M)
    inten = jnp.concatenate([inten, inten], 1)
    packed = jnp.concatenate([probe[0].reshape(M, M), probe[1].reshape(M, M)], 1)
    vmem = pl.BlockSpec(memory_space=pltpu.VMEM)
    smem = pl.BlockSpec(memory_space=pltpu.SMEM)
    anywhere = pl.BlockSpec(memory_space=pl.ANY)
    n_near = n_grp * n_zh
    dma = pltpu.SemaphoreType.DMA
    small = (NB, 3, ZB, 128)
    out, probe_grad = pl.pallas_call(
        functools.partial(kernel, sizes),
        out_shape=(
            jax.ShapeDtypeStruct((E, X, NB * ZB, 128), BF16),
            jax.ShapeDtypeStruct((M, 128), F32),
        ),
        in_specs=[
            anywhere,
            anywhere,
            vmem,
            smem,
            vmem,
            vmem,
            vmem,
            smem,
            smem,
            smem,
            vmem,
            vmem,
            vmem,
        ],
        out_specs=(anywhere, vmem),
        scratch_shapes=[
            pltpu.VMEM((E, NB, ZB * X, 128), BF16),
            pltpu.VMEM((E, NB, ZB * X, 128), F32),
            pltpu.VMEM((ZB * 128, C), BF16),
            pltpu.VMEM(small, F32),
            pltpu.VMEM(small, F32),
            pltpu.VMEM((NB, E, ZB, 128), F32),
            pltpu.VMEM((NB, E, ZB, 128), F32),
            pltpu.VMEM(small, F32),
            pltpu.VMEM(small, F32),
            pltpu.VMEM((NB, X, ZB, 128), F32),
            pltpu.VMEM((NB, 2, ZB, 128), F32),
            pltpu.VMEM((NB, 2, ZB, 128), F32),
            pltpu.VMEM(small, F32),
            pltpu.VMEM(small, F32),
            pltpu.VMEM((NB, 2, E, 8, 128), F32),
            pltpu.VMEM((ZB * E, 128), F32),
            pltpu.VMEM((E, ZB * 128), F32),
            pltpu.VMEM((E, X, NB * ZB, 128), BF16),
            pltpu.VMEM((128, 256), F32),
            pltpu.VMEM((2, M, 128), F32),
            pltpu.VMEM((NB, 8, 128), F32),
            pltpu.VMEM((NB, 8, 128), F32),
            pltpu.VMEM((n_near, 8, 128), F32),
            pltpu.VMEM((n_x, 8, 128), F32),
            pltpu.VMEM((NB, 8, 128), F32),
            dma((NB,)),
            dma,
            dma((NB,)),
            dma((NB,)),
            dma((NB,)),
            dma((NB,)),
            dma((NB,)),
            dma((NB,)),
            dma((NB,)),
            dma((NB,)),
            dma((NB,)),
            dma((NB,)),
            dma((NB,)),
            dma((14,)),
            dma((NB, 2)),
            dma((NB,)),
            dma((NB,)),
            dma((n_near,)),
            dma((n_near,)),
            dma((n_x,)),
            dma((n_x,)),
            dma((NB,)),
            dma((NB,)),
        ],
        compiler_params=pltpu.CompilerParams(
            collective_id=0, has_side_effects=True, vmem_limit_bytes=56 * 1024 * 1024
        ),
    )(
        dens,
        spec,
        inten,
        positions.reshape(2 * K),
        packed,
        line_channels.astype(F32),
        line_weights,
        atten_coef,
        beta_coef,
        delta_coef,
        jnp.asarray(chirps),
        jnp.asarray(right),
        jnp.asarray(left),
    )
    gradient = jnp.swapaxes(out, 1, 2)
    probe_grad = jnp.stack([probe_grad[:, :M].reshape(M * M), probe_grad[:, M:].reshape(M * M)])
    return gradient, probe_grad


def solution(mesh):
    n_grp, n_beam, n_row = mesh.shape["grp"], mesh.shape["beam"], mesh.shape["row"]
    n_zh = 4 if n_row % 4 == 0 else 1
    sizes = (n_grp, n_row, n_row // n_zh, n_zh, float(K * n_grp * n_beam * n_row))
    return jax.shard_map(
        functools.partial(body, sizes),
        mesh=mesh,
        in_specs=(
            P(None, "grp", "beam", "row"),
            P(("grp", "beam"), "row", None),
            P(("grp", "beam", "row"), None),
            P(("grp", "beam", "row"), None),
            P(),
            P(),
            P(),
            P(),
            P(),
            P(),
        ),
        out_specs=(P(None, "grp", "beam", "row"), P()),
        check_vma=False,
    )
```

```python
import functools
import math

import jax
import jax.numpy as jnp
import numpy as np
from jax import lax
from jax.experimental import pallas as pl
from jax.experimental.pallas import tpu as pltpu
from jax.sharding import PartitionSpec as P

E = 32
C = 512
M = 64
K = 32
X = 4
ZB = 16
NB = 8
GROUP = 16
ORDER = (4, 1, 7, 3, 5, 2, 6)
EARLY = 1
PART = 4

F32 = jnp.float32
BF16 = jnp.bfloat16
HIGHEST = lax.Precision.HIGHEST
MESH = pl.DeviceIdType.MESH
object_weight = 1000.0


def halves(values):
    high = values.astype(BF16)
    return high, (values - high.astype(F32)).astype(BF16)


def swap(values):
    return pltpu.roll(values, M, 1)


def matmul(left, right):
    return jnp.dot(left, right, preferred_element_type=F32)


def np_halves(values):
    high = values.astype(np.float32).astype(jnp.bfloat16)
    low = (values - high.astype(np.float64)).astype(np.float32).astype(jnp.bfloat16)
    return high, low


def constant_tables():
    index = np.arange(M)
    angles = 2.0 * math.pi / M * (index[:, None] * index[None, :] % M)
    dft_real = np.cos(angles) / math.sqrt(M)
    dft_imag = -np.sin(angles) / math.sqrt(M)
    centred = np.arange(M) - M // 2
    chirp = math.pi * 0.5 / M * (centred[:, None] ** 2 + centred[None, :] ** 2)
    chirp_real, chirp_imag = np.cos(chirp), np.sin(chirp)
    chirps = np.stack(
        [
            np.concatenate([chirp_real, chirp_real], 1),
            np.concatenate([-chirp_imag, chirp_imag], 1),
        ]
    ).astype(np.float32)

    def right_table(sign):
        table = np.block([[dft_real, sign * dft_imag], [-sign * dft_imag, dft_real]])
        high, low = np_halves(table)
        row = np.concatenate([high, low], 1)
        return np.concatenate([row, row], 0)

    right = np.stack([right_table(1.0), right_table(-1.0)])
    high, low = np_halves(np.concatenate([dft_real, dft_imag], 0))
    left = np.concatenate([high, high, low, low], 1)
    return chirps, right, left


def kernel(
    sizes,
    dens_hbm,
    spec_hbm,
    inten_hbm,
    pos_ref,
    probe_ref,
    chan_ref,
    weight_ref,
    atten_ref,
    beta_ref,
    delta_ref,
    chirp_ref,
    right_ref,
    left_ref,
    out_hbm,
    probe_out,
    dens_bf,
    dens_f,
    spec_v,
    inten_bf,
    inten_f,
    image_ref,
    tap_src,
    tap_rcv,
    u_src,
    u_rcv,
    ow_src,
    ow_rcv,
    inc_ref,
    tg_src,
    tg_rcv,
    lg_src,
    lg_rcv,
    eg_ref,
    mix_ref,
    fit_ref,
    out_v,
    tile_ref,
    pgsum_ref,
    pr_src,
    pr_rcv,
    pa_rcv,
    pb_rcv,
    pf_rcv,
    dens_sem,
    spec_sem,
    inten_sem,
    out_sem,
    tap_ss,
    tap_rs,
    u_ss,
    u_rs,
    ow_ss,
    ow_rs,
    tg_ss,
    tg_rs,
    lg_ss,
    lg_rs,
    eg_ss,
    eg_rs,
    pr_ss,
    pr_rs,
    pa_ss,
    pa_rs,
    pb_ss,
    pb_rs,
    pf_ss,
    pf_rs,
):
    n_grp, n_row, n_x, n_zh, total = sizes
    me = lax.axis_index("beam")
    grp = lax.axis_index("grp")
    row = lax.axis_index("row")
    row_x, row_z = row // n_zh, row % n_zh
    n_near = n_grp * n_zh
    near = grp * n_zh + row_z

    def near_id(step):
        other = (near + step) % n_near
        return {"grp": other // n_zh, "row": row_x * n_zh + other % n_zh}

    def x_id(step):
        return {"row": ((row_x + step) % n_x) * n_zh + row_z}

    def peer(step):
        return (me + step) % NB

    def remote(source, target, send, recv, device):
        return pltpu.make_async_remote_copy(
            src_ref=source,
            dst_ref=target,
            send_sem=send,
            recv_sem=recv,
            device_id=device,
            device_id_type=MESH,
        )

    barrier = pltpu.get_barrier_semaphore()
    for step in range(1, NB):
        pl.semaphore_signal(barrier, inc=1, device_id={"beam": peer(step)}, device_id_type=MESH)
    for step in range(1, n_near):
        pl.semaphore_signal(barrier, inc=1, device_id=near_id(step), device_id_type=MESH)
    for step in range(1, n_x):
        pl.semaphore_signal(barrier, inc=1, device_id=x_id(step), device_id_type=MESH)

    def dens_copy(step):
        block = (me + 1 + step) % NB
        return pltpu.make_async_copy(
            dens_hbm.at[:, block], dens_bf.at[:, block], dens_sem.at[step]
        )

    for step in range(NB):
        dens_copy(step).start()
    spec_copy = pltpu.make_async_copy(spec_hbm, spec_v, spec_sem)
    spec_copy.start()
    inten_copy = pltpu.make_async_copy(inten_hbm, inten_bf, inten_sem)
    inten_copy.start()

    def cell(e, block, x):
        return dens_f[e, block, pl.ds(x, ZB, stride=X), :]

    def project(step, carry):
        block = (me + 1 + step) % NB
        dens_copy(step).wait()
        dens_f[:, block] = dens_bf[:, block].astype(F32)

        def add(e, sums):
            cells = [cell(e, block, x) for x in range(X)]
            total_cells = (cells[0] + cells[1]) + (cells[2] + cells[3])
            optical = [sums[x] + atten_ref[e] * cells[x] for x in range(X)]
            return (
                *optical,
                sums[X] + beta_ref[e] * total_cells,
                sums[X + 1] + delta_ref[e] * total_cells,
            )

        zero = jnp.zeros((ZB, 128), F32)
        sums = lax.fori_loop(0, E, add, (zero,) * (X + 2), unroll=E)
        depth = zero
        for x in range(X):
            inc_ref[block, x] = jnp.exp(-depth)
            depth = depth + sums[x]
        tap_src[block, 0] = depth
        tap_src[block, 1] = sums[X]
        tap_src[block, 2] = sums[X + 1]

        return carry

    lax.fori_loop(0, NB, project, 0)
    pl.semaphore_wait(barrier, NB - 1 + n_near - 1 + n_x - 1)
    tap_sends, u_sends = [], []

    def send_tap(step):
        dst = peer(step)
        copy = remote(
            tap_src.at[dst], tap_rcv.at[me], tap_ss.at[step], tap_rs.at[me], {"beam": dst}
        )
        copy.start()
        tap_sends.append(copy)

    def send_u(step):
        dst = peer(step)
        copy = remote(u_src.at[dst], u_rcv.at[me], u_ss.at[step], u_rs.at[me], {"beam": dst})
        copy.start()
        u_sends.append(copy)

    for step in range(1, NB):
        send_tap(step)
    tap_rcv[me] = tap_src[me]

    def emit(step, carry):
        block = (me + 1 + step) % NB
        local = [inc_ref[block, x] for x in range(X)]

        def one(e, inner):
            terms = [cell(e, block, x) * local[x] for x in range(1, X)]
            u_src[block, e] = (cell(e, block, 0) + terms[0]) + (terms[1] + terms[2])
            return inner

        lax.fori_loop(0, E, one, 0, unroll=E)

        return carry

    lax.fori_loop(0, NB, emit, 0)
    for step in ORDER[:EARLY]:
        send_u(step)
    u_rcv[me] = u_src[me]

    for step in range(1, NB):
        src = peer(step)
        remote(tap_src.at[src], tap_rcv.at[src], tap_ss.at[0], tap_rs.at[src], {"beam": src}).wait_recv()
    before = jnp.zeros((ZB, 128), F32)
    absorb = jnp.zeros((ZB, 128), F32)
    phase = jnp.zeros((ZB, 128), F32)
    for d in range(NB):
        ow_src[d, 2] = jnp.exp(-before)
        before = before + tap_rcv[d, 0]
        absorb = absorb + tap_rcv[d, 1]
        phase = phase + tap_rcv[d, 2]
    amplitude = jnp.exp(-absorb)
    own_real = amplitude * jnp.cos(phase)
    own_imag = amplitude * jnp.sin(phase)
    for d in range(NB):
        ow_src[d, 0] = own_real
        ow_src[d, 1] = own_imag
    ow_sends = []
    for step in range(1, NB):
        dst = peer(step)
        copy = remote(
            ow_src.at[dst], ow_rcv.at[me], ow_ss.at[step], ow_rs.at[me], {"beam": dst}
        )
        copy.start()
        ow_sends.append(copy)
    ow_rcv[me] = ow_src[me]
    for step in ORDER[EARLY:]:
        send_u(step)

    eye = (
        lax.broadcasted_iota(jnp.int32, (E, E), 0) == lax.broadcasted_iota(jnp.int32, (E, E), 1)
    ).astype(F32)

    def columns_of(rows):
        return lax.dot_general(
            eye, rows, (((1,), (1,)), ((), ())), precision=HIGHEST, preferred_element_type=F32
        )

    lines = columns_of(chan_ref[...].astype(F32))
    strengths = columns_of(weight_ref[...])
    channel = lax.broadcasted_iota(jnp.int32, (E, C), 1).astype(F32)
    table = jnp.zeros((E, C), F32)
    for line in range(4):
        offset = channel - lines[:, line : line + 1]
        table = table + strengths[:, line : line + 1] * jnp.exp(-offset * offset / 8.0)
    gram = lax.dot_general(
        table, table, (((1,), (1,)), ((), ())), precision=HIGHEST, preferred_element_type=F32
    )
    gram_high, gram_low = halves(gram)
    gram_parts = jnp.concatenate([gram_high, gram_low], 0)

    spec_copy.wait()
    table_high, table_low = halves(table)
    fit = lax.dot_general(
        jnp.concatenate([table_high, table_low], 0),
        spec_v[...],
        (((1,), (1,)), ((), ())),
        preferred_element_type=F32,
    )
    fit_ref[...] = fit[:E] + fit[E:]

    lane = lax.broadcasted_iota(jnp.int32, (M, 128), 1)
    first = lane < M
    even = lax.broadcasted_iota(jnp.int32, (M, 128), 0) % 2 == 0
    inten_copy.wait()
    flat = inten_bf[...].astype(F32)
    for g in range(M // 2):
        group = flat[:, g * 128 : (g + 1) * 128]
        inten_f[pl.ds(2 * g, K, stride=M), :] = group
        inten_f[pl.ds(2 * g + 1, K, stride=M), :] = group
    for part in range(2):
        for g in range(M // 2):
            group = probe_ref[part : part + 1, g * 128 : (g + 1) * 128]
            image_ref[part, 2 * g : 2 * g + 1, :] = group
            image_ref[part, 2 * g + 1 : 2 * g + 2, :] = group
    image_real, image_imag = image_ref[0], image_ref[1]
    probe = jnp.where(
        first,
        jnp.where(even, image_real, swap(image_real)),
        jnp.where(even, swap(image_imag), image_imag),
    )
    keep = first == even

    for step in range(1, NB):
        src = peer(step)
        remote(ow_src.at[src], ow_rcv.at[src], ow_ss.at[0], ow_rs.at[src], {"beam": src}).wait_recv()

    illum = probe * chirp_ref[0] + swap(probe) * chirp_ref[1]
    illum_swap = swap(illum)
    illum_a = jnp.where(first, illum, illum_swap)
    illum_b = jnp.where(first, -illum_swap, illum)
    sign = jnp.where(first, -1.0, 1.0).astype(F32)

    obj_real = ow_rcv[:, 0].reshape(NB * ZB, 128)
    obj_imag = ow_rcv[:, 1].reshape(NB * ZB, 128)
    real_high, real_low = halves(obj_real)
    imag_high, imag_low = halves(obj_imag)
    field = jnp.concatenate([real_high, imag_high, real_low, imag_low], 1)

    pick_z = lax.broadcasted_iota(jnp.int32, (M, 128), 1) - lax.broadcasted_iota(
        jnp.int32, (M, 128), 0
    )
    gather_row = lax.broadcasted_iota(jnp.int32, (256, 128), 0)
    gather_col = lax.broadcasted_iota(jnp.int32, (256, 128), 1)
    pick_y = jnp.where(
        (gather_row < 128) == (gather_col < M), gather_row % 128 - gather_col % M, -1
    )
    spread_row = lax.broadcasted_iota(jnp.int32, (128, 256), 0)
    spread_col = lax.broadcasted_iota(jnp.int32, (128, 256), 1)
    place_y = jnp.where(
        (spread_col < 128) == (spread_row < M), spread_col % 128 - spread_row % M, -1
    )
    place_z = lax.broadcasted_iota(jnp.int32, (128, 128), 0) - (
        lax.broadcasted_iota(jnp.int32, (128, 128), 1) % M
    )

    tile_ref[...] = jnp.zeros(tile_ref.shape, F32)
    pgsum_ref[...] = jnp.zeros(pgsum_ref.shape, F32)

    def transform(values, right, conj):
        high, low = halves(values)
        product = matmul(jnp.concatenate([high, low], 1), right)
        product = product[:, :128] + product[:, 128:]
        high, low = halves(product)
        outs = []
        for i in range(GROUP):
            part = slice(i * M, (i + 1) * M)
            stack = jnp.concatenate([high[part], low[part], high[part], low[part]], 0)
            both = matmul(left_ref[...], stack)
            turned = swap(both[M:]) * sign
            outs.append(both[:M] - turned if conj else both[:M] + turned)
        return outs

    def positions_step(group, carry):
        windows, picks = [], []
        starts = [
            (pos_ref[0, group * GROUP + i], pos_ref[1, group * GROUP + i])
            for i in range(GROUP)
        ]
        for i in range(GROUP):
            rows = (pick_z == starts[i][0]).astype(F32).astype(BF16)
            cut = matmul(rows, field).astype(BF16)
            stack = jnp.concatenate([cut[:, :256], cut[:, 256:]], 0)
            columns = (pick_y == starts[i][1]).astype(F32).astype(BF16)
            both = matmul(stack, columns)
            windows.append(both[:M] + both[M:])
        exits = [w * illum_a + swap(w) * illum_b for w in windows]
        far = transform(jnp.concatenate(exits, 0), right_ref[0], False)
        pulled = []
        for i in range(GROUP):
            square = far[i] * far[i]
            start = pl.multiple_of((group * GROUP + i) * M, M)
            measured = inten_f[pl.ds(start, M), :]
            measured = jnp.where(keep, measured, swap(measured))
            misfit = square + swap(square) - measured
            pulled.append(misfit * far[i])
        back = transform(jnp.concatenate(pulled, 0), right_ref[1], True)
        sum_a = pgsum_ref[0]
        sum_b = pgsum_ref[1]
        tile = tile_ref[...]
        for i in range(GROUP):
            sum_a = sum_a + windows[i] * back[i]
            sum_b = sum_b + swap(windows[i]) * back[i]
            grad = back[i] * illum_a - swap(back[i]) * illum_b
            high, low = halves(grad)
            columns = (place_y == starts[i][1]).astype(F32).astype(BF16)
            spread = matmul(jnp.concatenate([high, low], 0), columns).astype(BF16)
            rows = (place_z == starts[i][0]).astype(F32).astype(BF16)
            tile = tile + matmul(rows, spread)
        pgsum_ref[0] = sum_a
        pgsum_ref[1] = sum_b
        tile_ref[...] = tile
        return carry

    lax.fori_loop(0, K // GROUP, positions_step, 0)

    for d in range(NB):
        tg_src[d, 0] = tile_ref[d * ZB : (d + 1) * ZB, :128]
        tg_src[d, 1] = tile_ref[d * ZB : (d + 1) * ZB, 128:]
    sum_a, sum_b = pgsum_ref[0], pgsum_ref[1]
    conj_sum = jnp.where(first, sum_a + swap(sum_a), sum_b - swap(sum_b))
    local_probe = conj_sum * chirp_ref[0] - swap(conj_sum) * chirp_ref[1]
    image_ref[0] = local_probe
    upper, lower = image_ref[0, pl.ds(0, M // 2, stride=2), :], image_ref[0, pl.ds(1, M // 2, stride=2), :]
    half_first = first[: M // 2]
    flat_real = jnp.where(half_first, upper, swap(lower))
    flat_imag = jnp.where(half_first, swap(upper), lower)
    for d in range(NB // 2):
        pr_src[d] = flat_real[d * 8 : (d + 1) * 8]
        pr_src[NB // 2 + d] = flat_imag[d * 8 : (d + 1) * 8]
    tg_sends, pr_sends = [], []
    for step in range(1, NB):
        dst = peer(step)
        copy = remote(
            tg_src.at[dst], tg_rcv.at[me], tg_ss.at[step], tg_rs.at[me], {"beam": dst}
        )
        copy.start()
        tg_sends.append(copy)
    for step in range(1, NB):
        dst = peer(step)
        copy = remote(
            pr_src.at[dst], pr_rcv.at[me], pr_ss.at[step], pr_rs.at[me], {"beam": dst}
        )
        copy.start()
        pr_sends.append(copy)
    tg_rcv[me] = tg_src[me]
    pr_rcv[me] = pr_src[me]

    def scale_block(block, carry):
        for x in range(X):
            inc_ref[block, x] = inc_ref[block, x] * ow_rcv[block, 2]
        return carry

    lax.fori_loop(0, NB, scale_block, 0)

    for step in range(1, NB):
        src = peer(step)
        remote(u_src.at[src], u_rcv.at[src], u_ss.at[0], u_rs.at[src], {"beam": src}).wait_recv()
    shield = [ow_src[d, 2] for d in range(NB)]

    def add_slabs(e, carry):
        value = u_rcv[0, e] * shield[0]
        for d in range(1, NB):
            value = value + u_rcv[d, e] * shield[d]
        mix_ref[pl.ds(e, ZB, stride=E), :] = value
        return carry

    lax.fori_loop(0, E, add_slabs, 0, unroll=E)
    columns = jnp.concatenate([mix_ref[z * E : (z + 1) * E, :] for z in range(ZB)], 1)
    high, low = halves(columns)
    product = matmul(gram_parts, jnp.concatenate([high, low], 1))
    product = product[:E] + product[E:]
    grads = (product[:, : ZB * 128] + product[:, ZB * 128 :]) - fit_ref[...]
    for z in range(ZB):
        mix_ref[z * E : (z + 1) * E, :] = grads[:, z * 128 : (z + 1) * 128]

    def to_layers(e, carry):
        value = mix_ref[pl.ds(e, ZB, stride=E), :]
        eg_ref[me, 0, e] = value[:8]
        eg_ref[me, 1, e] = value[8:]
        return carry

    lax.fori_loop(0, E, to_layers, 0, unroll=E)

    beam_z, beam_y = me // 4, me % 4
    up = beam_z * 4 + (beam_y + 1) % 4
    down = beam_z * 4 + (beam_y + 3) % 4
    across = (1 - beam_z) * 4 + beam_y
    far_side = beam_z * 4 + (beam_y + 2) % 4
    across_up = (1 - beam_z) * 4 + (beam_y + 1) % 4
    across_down = (1 - beam_z) * 4 + (beam_y + 3) % 4
    across_far = (1 - beam_z) * 4 + (beam_y + 2) % 4

    eg_sends = []

    def hand(block, half, dst):
        copy = remote(
            eg_ref.at[block, half],
            eg_ref.at[block, half],
            eg_ss.at[len(eg_sends)],
            eg_rs.at[block, half],
            {"beam": dst},
        )
        copy.start()
        eg_sends.append(copy)

    def arrive(block, half):
        remote(
            eg_ref.at[block, half],
            eg_ref.at[block, half],
            eg_ss.at[0],
            eg_rs.at[block, half],
            {"beam": block},
        ).wait_recv()

    hand(me, 0, up)
    hand(me, 1, down)
    hand(me, 0, across)
    hand(me, 1, across)
    hand(me, 1, up)
    hand(me, 0, down)

    for step in range(1, NB):
        src = peer(step)
        remote(pr_src.at[src], pr_rcv.at[src], pr_ss.at[0], pr_rs.at[src], {"beam": src}).wait_recv()
    piece = pr_rcv[0]
    for d in range(1, NB):
        piece = piece + pr_rcv[d]
    pa_rcv[near] = piece
    pa_sends = []
    for step in range(1, n_near):
        copy = remote(
            pa_rcv.at[near], pa_rcv.at[near], pa_ss.at[step], pa_rs.at[near], near_id(step)
        )
        copy.start()
        pa_sends.append(copy)

    def weigh(e, sums):
        value = jnp.concatenate([eg_ref[me, 0, e], eg_ref[me, 1, e]], 0)
        return tuple(sums[d] + value * u_rcv[d, e] for d in range(NB))

    weighted = lax.fori_loop(0, E, weigh, (jnp.zeros((ZB, 128), F32),) * NB, unroll=8)

    for step in range(1, NB):
        src = peer(step)
        remote(tg_src.at[src], tg_rcv.at[src], tg_ss.at[0], tg_rs.at[src], {"beam": src}).wait_recv()
    tile_real = tg_rcv[0, 0]
    tile_imag = tg_rcv[0, 1]
    for d in range(1, NB):
        tile_real = tile_real + tg_rcv[d, 0]
        tile_imag = tile_imag + tg_rcv[d, 1]
    own_real, own_imag = ow_src[0, 0], ow_src[0, 1]
    grad_absorb = -object_weight * (own_real * tile_real + own_imag * tile_imag)
    grad_phase = object_weight * (own_real * tile_imag - own_imag * tile_real)
    later = jnp.zeros((ZB, 128), F32)
    for d in range(NB - 1, -1, -1):
        lg_src[d, 0] = later
        lg_src[d, 1] = grad_absorb
        lg_src[d, 2] = grad_phase
        later = later + weighted[d] * shield[d]
    lg_sends = []
    for step in range(1, NB):
        dst = peer(step)
        copy = remote(
            lg_src.at[dst], lg_rcv.at[me], lg_ss.at[step], lg_rs.at[me], {"beam": dst}
        )
        copy.start()
        lg_sends.append(copy)
    lg_rcv[me] = lg_src[me]

    def out_copy(order, block):
        return pltpu.make_async_copy(
            out_v.at[:, block], out_hbm.at[:, block], out_sem.at[order]
        )

    def finish(order, block):
        def grad_of(e):
            return jnp.concatenate([eg_ref[block, 0, e], eg_ref[block, 1, e]], 0)

        def weigh_cells(e, sums):
            value = grad_of(e)
            return tuple(sums[x] + value * cell(e, block, x) for x in range(X))

        zero = jnp.zeros((ZB, 128), F32)
        sums = lax.fori_loop(0, E, weigh_cells, (zero,) * X, unroll=E)
        light = [inc_ref[block, x] for x in range(X)]
        beyond = [None] * X
        running = lg_rcv[block, 0]
        for x in range(X - 1, -1, -1):
            beyond[x] = running
            running = running + light[x] * sums[x]
        absorb_grad, phase_grad = lg_rcv[block, 1], lg_rcv[block, 2]

        def write(e, carry):
            value = grad_of(e)
            shared = beta_ref[e] * absorb_grad + delta_ref[e] * phase_grad
            for x in range(X):
                result = value * light[x] - atten_ref[e] * beyond[x] + shared
                dens_f[e, block, pl.ds(x, ZB, stride=X), :] = result
            out_v[e, block] = dens_f[e, block].astype(BF16)
            return carry

        lax.fori_loop(0, E, write, 0, unroll=E)
        out_copy(order, block).start()

    def extras(block):
        remote(lg_src.at[block], lg_rcv.at[block], lg_ss.at[0], lg_rs.at[block], {"beam": block}).wait_recv()

    arrive(down, 0)
    hand(down, 0, up)
    arrive(up, 1)
    hand(up, 1, down)
    arrive(across, 0)
    hand(across, 0, up)
    hand(across, 0, down)
    finish(0, me)
    arrive(across, 1)
    hand(across, 1, up)
    hand(across, 1, down)

    for step in range(1, n_near):
        src = (near + step) % n_near
        remote(pa_rcv.at[src], pa_rcv.at[src], pa_ss.at[0], pa_rs.at[src], near_id(step)).wait_recv()
    piece = pa_rcv[0]
    for d in range(1, n_near):
        piece = piece + pa_rcv[d]
    pb_rcv[row_x] = piece
    pb_sends = []
    for step in range(1, n_x):
        copy = remote(
            pb_rcv.at[row_x], pb_rcv.at[row_x], pb_ss.at[step], pb_rs.at[row_x], x_id(step)
        )
        copy.start()
        pb_sends.append(copy)

    arrive(down, 1)
    extras(down)
    finish(1, down)
    arrive(far_side, 0)
    hand(far_side, 0, across)
    arrive(far_side, 1)
    hand(far_side, 1, across)
    arrive(up, 0)
    extras(up)
    finish(2, up)
    extras(across)
    finish(3, across)

    for step in range(1, n_x):
        src = (row_x + step) % n_x
        remote(pb_rcv.at[src], pb_rcv.at[src], pb_ss.at[0], pb_rs.at[src], x_id(step)).wait_recv()
    piece = pb_rcv[0]
    for d in range(1, n_x):
        piece = piece + pb_rcv[d]
    pf_rcv[me] = piece * (1.0 / total)
    pf_sends = []
    for step in range(1, NB):
        copy = remote(
            pf_rcv.at[me], pf_rcv.at[me], pf_ss.at[step], pf_rs.at[me], {"beam": peer(step)}
        )
        copy.start()
        pf_sends.append(copy)

    extras(far_side)
    finish(4, far_side)
    arrive(across_up, 0)
    arrive(across_up, 1)
    extras(across_up)
    finish(5, across_up)
    arrive(across_down, 0)
    arrive(across_down, 1)
    extras(across_down)
    finish(6, across_down)
    for step in range(1, NB):
        src = peer(step)
        remote(pf_rcv.at[src], pf_rcv.at[src], pf_ss.at[0], pf_rs.at[src], {"beam": src}).wait_recv()
    for d in range(NB):
        for g in range(8):
            start = (d % 4 * 8 + g) * 128
            probe_out[d // 4 : d // 4 + 1, start : start + 128] = pf_rcv[d, g : g + 1, :]
    arrive(across_far, 0)
    arrive(across_far, 1)
    extras(across_far)
    finish(7, across_far)

    for copy in tap_sends + u_sends + ow_sends + tg_sends + pr_sends + pa_sends + eg_sends + lg_sends + pb_sends + pf_sends:
        copy.wait_send()
    for order, block in enumerate(
        [me, down, up, across, far_side, across_up, across_down, across_far]
    ):
        out_copy(order, block).wait()


def hand_over(grad_hbm, probe_hbm, grad_out, probe_out, grad_v, probe_v, in_sems, out_sems):
    count = E // PART
    loads, stores = [], []
    for part in range(count):
        rows = pl.ds(part * PART, PART)
        loads.append(
            pltpu.make_async_copy(grad_hbm.at[rows], grad_v.at[rows], in_sems.at[part])
        )
        stores.append(
            pltpu.make_async_copy(grad_v.at[rows], grad_out.at[rows], out_sems.at[part])
        )
    loads.append(pltpu.make_async_copy(probe_hbm, probe_v, in_sems.at[count]))
    stores.append(pltpu.make_async_copy(probe_v, probe_out, out_sems.at[count]))
    for load in loads:
        load.start()
    for load, store in zip(loads, stores):
        load.wait()
        store.start()
    for store in stores:
        store.wait()


def body(
    sizes,
    densities,
    spectra,
    intensities,
    positions,
    probe,
    line_channels,
    line_weights,
    atten_coef,
    beta_coef,
    delta_coef,
):
    n_grp, n_row, n_x, n_zh, total = sizes
    chirps, right, left = constant_tables()
    dens = densities.reshape(E, NB, ZB * X, 128)
    spec = spectra.reshape(ZB * 128, C)
    vmem = pl.BlockSpec(memory_space=pltpu.VMEM)
    smem = pl.BlockSpec(memory_space=pltpu.SMEM)
    anywhere = pl.BlockSpec(memory_space=pl.ANY)
    n_near = n_grp * n_zh
    dma = pltpu.SemaphoreType.DMA
    small = (NB, 3, ZB, 128)
    out, probe_grad = pl.pallas_call(
        functools.partial(kernel, sizes),
        out_shape=(
            jax.ShapeDtypeStruct((E, NB, ZB * X, 128), BF16),
            jax.ShapeDtypeStruct((2, M * M), F32),
        ),
        in_specs=[
            anywhere,
            anywhere,
            anywhere,
            smem,
            vmem,
            vmem,
            vmem,
            smem,
            smem,
            smem,
            vmem,
            vmem,
            vmem,
        ],
        out_specs=(anywhere, vmem),
        scratch_shapes=[
            pltpu.VMEM((E, NB, ZB * X, 128), BF16),
            pltpu.VMEM((E, NB, ZB * X, 128), F32),
            pltpu.VMEM((ZB * 128, C), BF16),
            pltpu.VMEM((K, M * M), BF16),
            pltpu.VMEM((K * M, 128), F32),
            pltpu.VMEM((2, M, 128), F32),
            pltpu.VMEM(small, F32),
            pltpu.VMEM(small, F32),
            pltpu.VMEM((NB, E, ZB, 128), F32),
            pltpu.VMEM((NB, E, ZB, 128), F32),
            pltpu.VMEM(small, F32),
            pltpu.VMEM(small, F32),
            pltpu.VMEM((NB, X, ZB, 128), F32),
            pltpu.VMEM((NB, 2, ZB, 128), F32),
            pltpu.VMEM((NB, 2, ZB, 128), F32),
            pltpu.VMEM(small, F32),
            pltpu.VMEM(small, F32),
            pltpu.VMEM((NB, 2, E, 8, 128), F32),
            pltpu.VMEM((ZB * E, 128), F32),
            pltpu.VMEM((E, ZB * 128), F32),
            pltpu.VMEM((E, NB, ZB * X, 128), BF16),
            pltpu.VMEM((128, 256), F32),
            pltpu.VMEM((2, M, 128), F32),
            pltpu.VMEM((NB, 8, 128), F32),
            pltpu.VMEM((NB, 8, 128), F32),
            pltpu.VMEM((n_near, 8, 128), F32),
            pltpu.VMEM((n_x, 8, 128), F32),
            pltpu.VMEM((NB, 8, 128), F32),
            dma((NB,)),
            dma,
            dma,
            dma((NB,)),
            dma((NB,)),
            dma((NB,)),
            dma((NB,)),
            dma((NB,)),
            dma((NB,)),
            dma((NB,)),
            dma((NB,)),
            dma((NB,)),
            dma((NB,)),
            dma((NB,)),
            dma((14,)),
            dma((NB, 2)),
            dma((NB,)),
            dma((NB,)),
            dma((n_near,)),
            dma((n_near,)),
            dma((n_x,)),
            dma((n_x,)),
            dma((NB,)),
            dma((NB,)),
        ],
        compiler_params=pltpu.CompilerParams(
            collective_id=0, has_side_effects=True, vmem_limit_bytes=60 * 1024 * 1024
        ),
    )(
        dens,
        spec,
        intensities,
        positions.T,
        probe,
        line_channels.T,
        line_weights.T,
        atten_coef,
        beta_coef,
        delta_coef,
        jnp.asarray(chirps),
        jnp.asarray(right),
        jnp.asarray(left),
    )
    out, probe_grad = pl.pallas_call(
        hand_over,
        out_shape=(
            jax.ShapeDtypeStruct(out.shape, BF16),
            jax.ShapeDtypeStruct(probe_grad.shape, F32),
        ),
        in_specs=[anywhere, anywhere],
        out_specs=(anywhere, anywhere),
        scratch_shapes=[
            pltpu.VMEM(out.shape, BF16),
            pltpu.VMEM(probe_grad.shape, F32),
            dma((E // PART + 1,)),
            dma((E // PART + 1,)),
        ],
        compiler_params=pltpu.CompilerParams(vmem_limit_bytes=60 * 1024 * 1024),
    )(out, probe_grad)
    return out.reshape(densities.shape), probe_grad


def solution(mesh):
    n_grp, n_beam, n_row = mesh.shape["grp"], mesh.shape["beam"], mesh.shape["row"]
    n_zh = 4 if n_row % 4 == 0 else 1
    sizes = (n_grp, n_row, n_row // n_zh, n_zh, float(K * n_grp * n_beam * n_row))
    return jax.shard_map(
        functools.partial(body, sizes),
        mesh=mesh,
        in_specs=(
            P(None, "grp", "beam", "row"),
            P(("grp", "beam"), "row", None),
            P(("grp", "beam", "row"), None),
            P(("grp", "beam", "row"), None),
            P(),
            P(),
            P(),
            P(),
            P(),
            P(),
        ),
        out_specs=(P(None, "grp", "beam", "row"), P()),
        check_vma=False,
    )
```

```python
import functools
import math

import jax
import jax.numpy as jnp
import numpy as np
from jax import lax
from jax.experimental import pallas as pl
from jax.experimental.pallas import tpu as pltpu
from jax.sharding import PartitionSpec as P

E = 32
C = 512
M = 64
K = 32
X = 4
ZB = 16
NB = 8
GROUP = 16
NEAREST = (4, 1, 7, 3, 5, 2, 6)
ORDER = tuple((step, half) for half in range(2) for step in NEAREST)
EARLY = 3
PART = 4

F32 = jnp.float32
BF16 = jnp.bfloat16
HIGHEST = lax.Precision.HIGHEST
MESH = pl.DeviceIdType.MESH
object_weight = 1000.0


def halves(values):
    high = values.astype(BF16)
    return high, (values - high.astype(F32)).astype(BF16)


def swap(values):
    return pltpu.roll(values, M, 1)


def matmul(left, right):
    return jnp.dot(left, right, preferred_element_type=F32)


def np_halves(values):
    high = values.astype(np.float32).astype(jnp.bfloat16)
    low = (values - high.astype(np.float64)).astype(np.float32).astype(jnp.bfloat16)
    return high, low


def constant_tables():
    index = np.arange(M)
    angles = 2.0 * math.pi / M * (index[:, None] * index[None, :] % M)
    dft_real = np.cos(angles) / math.sqrt(M)
    dft_imag = -np.sin(angles) / math.sqrt(M)
    centred = np.arange(M) - M // 2
    chirp = math.pi * 0.5 / M * (centred[:, None] ** 2 + centred[None, :] ** 2)
    chirp_real, chirp_imag = np.cos(chirp), np.sin(chirp)
    chirps = np.stack(
        [
            np.concatenate([chirp_real, chirp_real], 1),
            np.concatenate([-chirp_imag, chirp_imag], 1),
        ]
    ).astype(np.float32)

    def right_table(sign):
        table = np.block([[dft_real, sign * dft_imag], [-sign * dft_imag, dft_real]])
        high, low = np_halves(table)
        row = np.concatenate([high, low], 1)
        return np.concatenate([row, row], 0)

    right = np.stack([right_table(1.0), right_table(-1.0)])
    high, low = np_halves(np.concatenate([dft_real, dft_imag], 0))
    left = np.concatenate([high, high, low, low], 1)
    return chirps, right, left


def kernel(
    sizes,
    dens_hbm,
    spec_hbm,
    inten_hbm,
    pos_ref,
    probe_ref,
    chan_ref,
    weight_ref,
    atten_ref,
    beta_ref,
    delta_ref,
    chirp_ref,
    right_ref,
    left_ref,
    out_hbm,
    probe_out,
    dens_bf,
    dens_f,
    spec_v,
    inten_bf,
    inten_f,
    image_ref,
    tap_src,
    tap_rcv,
    u_src,
    u_rcv,
    ow_src,
    ow_rcv,
    inc_ref,
    tg_src,
    tg_rcv,
    lg_src,
    lg_rcv,
    eg_ref,
    mix_ref,
    fit_ref,
    out_v,
    tile_ref,
    pgsum_ref,
    pr_src,
    pr_rcv,
    pa_rcv,
    pb_rcv,
    pf_rcv,
    dens_sem,
    spec_sem,
    inten_sem,
    out_sem,
    tap_ss,
    tap_rs,
    u_ss,
    u_rs,
    ow_ss,
    ow_rs,
    tg_ss,
    tg_rs,
    lg_ss,
    lg_rs,
    eg_ss,
    eg_rs,
    pr_ss,
    pr_rs,
    pa_ss,
    pa_rs,
    pb_ss,
    pb_rs,
    pf_ss,
    pf_rs,
):
    n_grp, n_row, n_x, n_zh, total = sizes
    me = lax.axis_index("beam")
    grp = lax.axis_index("grp")
    row = lax.axis_index("row")
    row_x, row_z = row // n_zh, row % n_zh
    n_near = n_grp * n_zh
    near = grp * n_zh + row_z

    def near_id(step):
        other = (near + step) % n_near
        return {"grp": other // n_zh, "row": row_x * n_zh + other % n_zh}

    def x_id(step):
        return {"row": ((row_x + step) % n_x) * n_zh + row_z}

    def peer(step):
        return (me + step) % NB

    def remote(source, target, send, recv, device):
        return pltpu.make_async_remote_copy(
            src_ref=source,
            dst_ref=target,
            send_sem=send,
            recv_sem=recv,
            device_id=device,
            device_id_type=MESH,
        )

    barrier = pltpu.get_barrier_semaphore()
    for step in range(1, NB):
        pl.semaphore_signal(barrier, inc=1, device_id={"beam": peer(step)}, device_id_type=MESH)
    for step in range(1, n_near):
        pl.semaphore_signal(barrier, inc=1, device_id=near_id(step), device_id_type=MESH)
    for step in range(1, n_x):
        pl.semaphore_signal(barrier, inc=1, device_id=x_id(step), device_id_type=MESH)

    def dens_copy(step):
        block = (me + 1 + step) % NB
        return pltpu.make_async_copy(
            dens_hbm.at[:, block], dens_bf.at[:, block], dens_sem.at[step]
        )

    for step in range(NB):
        dens_copy(step).start()
    spec_copy = pltpu.make_async_copy(spec_hbm, spec_v, spec_sem)
    spec_copy.start()
    inten_copy = pltpu.make_async_copy(inten_hbm, inten_bf, inten_sem)
    inten_copy.start()

    def cell(e, block, x):
        return dens_f[e, block, pl.ds(x, ZB, stride=X), :]

    def project(step, carry):
        block = (me + 1 + step) % NB
        dens_copy(step).wait()
        dens_f[:, block] = dens_bf[:, block].astype(F32)

        def add(e, sums):
            cells = [cell(e, block, x) for x in range(X)]
            total_cells = (cells[0] + cells[1]) + (cells[2] + cells[3])
            optical = [sums[x] + atten_ref[e] * cells[x] for x in range(X)]
            return (
                *optical,
                sums[X] + beta_ref[e] * total_cells,
                sums[X + 1] + delta_ref[e] * total_cells,
            )

        zero = jnp.zeros((ZB, 128), F32)
        sums = lax.fori_loop(0, E, add, (zero,) * (X + 2), unroll=E)
        depth = zero
        for x in range(X):
            inc_ref[block, x] = jnp.exp(-depth)
            depth = depth + sums[x]
        tap_src[block, 0] = depth
        tap_src[block, 1] = sums[X]
        tap_src[block, 2] = sums[X + 1]

        return carry

    lax.fori_loop(0, NB, project, 0)
    pl.semaphore_wait(barrier, NB - 1 + n_near - 1 + n_x - 1)
    tap_sends, u_sends = [], []

    def send_tap(step):
        dst = peer(step)
        copy = remote(
            tap_src.at[dst], tap_rcv.at[me], tap_ss.at[step], tap_rs.at[me], {"beam": dst}
        )
        copy.start()
        tap_sends.append(copy)

    def u_copy(step, half):
        dst = peer(step)
        return remote(
            u_src.at[dst, half],
            u_rcv.at[me, half],
            u_ss.at[step, half],
            u_rs.at[me, half],
            {"beam": dst},
        )

    def send_u(step, half):
        copy = u_copy(step, half)
        copy.start()
        u_sends.append(copy)

    def wait_u(half):
        for step in range(1, NB):
            src = peer(step)
            remote(
                u_src.at[src, half],
                u_rcv.at[src, half],
                u_ss.at[step, half],
                u_rs.at[src, half],
                {"beam": src},
            ).wait_recv()

    for step in range(1, NB):
        send_tap(step)
    tap_rcv[me] = tap_src[me]

    def emit(step, carry):
        block = (me + 1 + step) % NB
        local = [inc_ref[block, x] for x in range(X)]

        def one(e, inner):
            terms = [cell(e, block, x) * local[x] for x in range(1, X)]
            value = (cell(e, block, 0) + terms[0]) + (terms[1] + terms[2])
            u_src[block, 0, e] = value[:8]
            u_src[block, 1, e] = value[8:]
            return inner

        lax.fori_loop(0, E, one, 0, unroll=E)

        return carry

    lax.fori_loop(0, NB, emit, 0)
    for step, half in ORDER[:EARLY]:
        send_u(step, half)
    u_rcv[me] = u_src[me]

    for step in range(1, NB):
        src = peer(step)
        remote(tap_src.at[src], tap_rcv.at[src], tap_ss.at[0], tap_rs.at[src], {"beam": src}).wait_recv()
    before = jnp.zeros((ZB, 128), F32)
    absorb = jnp.zeros((ZB, 128), F32)
    phase = jnp.zeros((ZB, 128), F32)
    for d in range(NB):
        ow_src[d, 2] = jnp.exp(-before)
        before = before + tap_rcv[d, 0]
        absorb = absorb + tap_rcv[d, 1]
        phase = phase + tap_rcv[d, 2]
    amplitude = jnp.exp(-absorb)
    own_real = amplitude * jnp.cos(phase)
    own_imag = amplitude * jnp.sin(phase)
    for d in range(NB):
        ow_src[d, 0] = own_real
        ow_src[d, 1] = own_imag
    ow_sends = []
    for step in range(1, NB):
        dst = peer(step)
        copy = remote(
            ow_src.at[dst], ow_rcv.at[me], ow_ss.at[step], ow_rs.at[me], {"beam": dst}
        )
        copy.start()
        ow_sends.append(copy)
    ow_rcv[me] = ow_src[me]
    for step, half in ORDER[EARLY:]:
        send_u(step, half)

    eye = (
        lax.broadcasted_iota(jnp.int32, (E, E), 0) == lax.broadcasted_iota(jnp.int32, (E, E), 1)
    ).astype(F32)

    def columns_of(rows):
        return lax.dot_general(
            eye, rows, (((1,), (1,)), ((), ())), precision=HIGHEST, preferred_element_type=F32
        )

    lines = columns_of(chan_ref[...].astype(F32))
    strengths = columns_of(weight_ref[...])
    channel = lax.broadcasted_iota(jnp.int32, (E, C), 1).astype(F32)
    table = jnp.zeros((E, C), F32)
    for line in range(4):
        offset = channel - lines[:, line : line + 1]
        table = table + strengths[:, line : line + 1] * jnp.exp(-offset * offset / 8.0)
    gram = lax.dot_general(
        table, table, (((1,), (1,)), ((), ())), precision=HIGHEST, preferred_element_type=F32
    )
    gram_high, gram_low = halves(gram)
    gram_parts = jnp.concatenate([gram_high, gram_low], 0)

    spec_copy.wait()
    table_high, table_low = halves(table)
    fit = lax.dot_general(
        jnp.concatenate([table_high, table_low], 0),
        spec_v[...],
        (((1,), (1,)), ((), ())),
        preferred_element_type=F32,
    )
    fit_ref[...] = fit[:E] + fit[E:]

    lane = lax.broadcasted_iota(jnp.int32, (M, 128), 1)
    first = lane < M
    even = lax.broadcasted_iota(jnp.int32, (M, 128), 0) % 2 == 0
    inten_copy.wait()
    flat = inten_bf[...].astype(F32)
    for g in range(M // 2):
        group = flat[:, g * 128 : (g + 1) * 128]
        inten_f[pl.ds(2 * g, K, stride=M), :] = group
        inten_f[pl.ds(2 * g + 1, K, stride=M), :] = group
    for part in range(2):
        for g in range(M // 2):
            group = probe_ref[part : part + 1, g * 128 : (g + 1) * 128]
            image_ref[part, 2 * g : 2 * g + 1, :] = group
            image_ref[part, 2 * g + 1 : 2 * g + 2, :] = group
    image_real, image_imag = image_ref[0], image_ref[1]
    probe = jnp.where(
        first,
        jnp.where(even, image_real, swap(image_real)),
        jnp.where(even, swap(image_imag), image_imag),
    )
    keep = first == even

    for step in range(1, NB):
        src = peer(step)
        remote(ow_src.at[src], ow_rcv.at[src], ow_ss.at[0], ow_rs.at[src], {"beam": src}).wait_recv()

    illum = probe * chirp_ref[0] + swap(probe) * chirp_ref[1]
    illum_swap = swap(illum)
    illum_a = jnp.where(first, illum, illum_swap)
    illum_b = jnp.where(first, -illum_swap, illum)
    sign = jnp.where(first, -1.0, 1.0).astype(F32)

    obj_real = ow_rcv[:, 0].reshape(NB * ZB, 128)
    obj_imag = ow_rcv[:, 1].reshape(NB * ZB, 128)
    real_high, real_low = halves(obj_real)
    imag_high, imag_low = halves(obj_imag)
    field = jnp.concatenate([real_high, imag_high, real_low, imag_low], 1)

    pick_z = lax.broadcasted_iota(jnp.int32, (M, 128), 1) - lax.broadcasted_iota(
        jnp.int32, (M, 128), 0
    )
    gather_row = lax.broadcasted_iota(jnp.int32, (256, 128), 0)
    gather_col = lax.broadcasted_iota(jnp.int32, (256, 128), 1)
    pick_y = jnp.where(
        (gather_row < 128) == (gather_col < M), gather_row % 128 - gather_col % M, -1
    )
    spread_row = lax.broadcasted_iota(jnp.int32, (128, 256), 0)
    spread_col = lax.broadcasted_iota(jnp.int32, (128, 256), 1)
    place_y = jnp.where(
        (spread_col < 128) == (spread_row < M), spread_col % 128 - spread_row % M, -1
    )
    place_z = lax.broadcasted_iota(jnp.int32, (128, 128), 0) - (
        lax.broadcasted_iota(jnp.int32, (128, 128), 1) % M
    )

    tile_ref[...] = jnp.zeros(tile_ref.shape, F32)
    pgsum_ref[...] = jnp.zeros(pgsum_ref.shape, F32)

    def transform(values, right, conj):
        high, low = halves(values)
        product = matmul(jnp.concatenate([high, low], 1), right)
        product = product[:, :128] + product[:, 128:]
        high, low = halves(product)
        outs = []
        for i in range(GROUP):
            part = slice(i * M, (i + 1) * M)
            stack = jnp.concatenate([high[part], low[part], high[part], low[part]], 0)
            both = matmul(left_ref[...], stack)
            turned = swap(both[M:]) * sign
            outs.append(both[:M] - turned if conj else both[:M] + turned)
        return outs

    def positions_step(group, carry):
        windows, picks = [], []
        starts = [
            (pos_ref[0, group * GROUP + i], pos_ref[1, group * GROUP + i])
            for i in range(GROUP)
        ]
        for i in range(GROUP):
            rows = (pick_z == starts[i][0]).astype(F32).astype(BF16)
            cut = matmul(rows, field).astype(BF16)
            stack = jnp.concatenate([cut[:, :256], cut[:, 256:]], 0)
            columns = (pick_y == starts[i][1]).astype(F32).astype(BF16)
            both = matmul(stack, columns)
            windows.append(both[:M] + both[M:])
        exits = [w * illum_a + swap(w) * illum_b for w in windows]
        far = transform(jnp.concatenate(exits, 0), right_ref[0], False)
        pulled = []
        for i in range(GROUP):
            square = far[i] * far[i]
            start = pl.multiple_of((group * GROUP + i) * M, M)
            measured = inten_f[pl.ds(start, M), :]
            measured = jnp.where(keep, measured, swap(measured))
            misfit = square + swap(square) - measured
            pulled.append(misfit * far[i])
        back = transform(jnp.concatenate(pulled, 0), right_ref[1], True)
        sum_a = pgsum_ref[0]
        sum_b = pgsum_ref[1]
        tile = tile_ref[...]
        for i in range(GROUP):
            sum_a = sum_a + windows[i] * back[i]
            sum_b = sum_b + swap(windows[i]) * back[i]
            grad = back[i] * illum_a - swap(back[i]) * illum_b
            high, low = halves(grad)
            columns = (place_y == starts[i][1]).astype(F32).astype(BF16)
            spread = matmul(jnp.concatenate([high, low], 0), columns).astype(BF16)
            rows = (place_z == starts[i][0]).astype(F32).astype(BF16)
            tile = tile + matmul(rows, spread)
        pgsum_ref[0] = sum_a
        pgsum_ref[1] = sum_b
        tile_ref[...] = tile
        return carry

    lax.fori_loop(0, K // GROUP, positions_step, 0)

    for d in range(NB):
        tg_src[d, 0] = tile_ref[d * ZB : (d + 1) * ZB, :128]
        tg_src[d, 1] = tile_ref[d * ZB : (d + 1) * ZB, 128:]
    sum_a, sum_b = pgsum_ref[0], pgsum_ref[1]
    conj_sum = jnp.where(first, sum_a + swap(sum_a), sum_b - swap(sum_b))
    local_probe = conj_sum * chirp_ref[0] - swap(conj_sum) * chirp_ref[1]
    image_ref[0] = local_probe
    upper, lower = image_ref[0, pl.ds(0, M // 2, stride=2), :], image_ref[0, pl.ds(1, M // 2, stride=2), :]
    half_first = first[: M // 2]
    flat_real = jnp.where(half_first, upper, swap(lower))
    flat_imag = jnp.where(half_first, swap(upper), lower)
    for d in range(NB // 2):
        pr_src[d] = flat_real[d * 8 : (d + 1) * 8]
        pr_src[NB // 2 + d] = flat_imag[d * 8 : (d + 1) * 8]
    tg_sends, pr_sends = [], []
    for step in range(1, NB):
        dst = peer(step)
        copy = remote(
            tg_src.at[dst], tg_rcv.at[me], tg_ss.at[step], tg_rs.at[me], {"beam": dst}
        )
        copy.start()
        tg_sends.append(copy)
    for step in range(1, NB):
        dst = peer(step)
        copy = remote(
            pr_src.at[dst], pr_rcv.at[me], pr_ss.at[step], pr_rs.at[me], {"beam": dst}
        )
        copy.start()
        pr_sends.append(copy)
    tg_rcv[me] = tg_src[me]
    pr_rcv[me] = pr_src[me]

    def scale_block(block, carry):
        for x in range(X):
            inc_ref[block, x] = inc_ref[block, x] * ow_rcv[block, 2]
        return carry

    lax.fori_loop(0, NB, scale_block, 0)

    shield = [ow_src[d, 2] for d in range(NB)]

    def own_half(half):
        rows = slice(half * 8, half * 8 + 8)
        count = E * 8

        def add_slabs(e, carry):
            value = u_rcv[0, half, e] * shield[0][rows]
            for d in range(1, NB):
                value = value + u_rcv[d, half, e] * shield[d][rows]
            mix_ref[pl.ds(half * count + e, 8, stride=E), :] = value
            return carry

        lax.fori_loop(0, E, add_slabs, 0, unroll=E)
        columns = jnp.concatenate(
            [mix_ref[half * count + z * E : half * count + (z + 1) * E, :] for z in range(8)], 1
        )
        high, low = halves(columns)
        product = matmul(gram_parts, jnp.concatenate([high, low], 1))
        product = product[:E] + product[E:]
        grads = (product[:, :1024] + product[:, 1024:]) - fit_ref[:, half * 1024 : half * 1024 + 1024]
        for z in range(8):
            mix_ref[half * count + z * E : half * count + (z + 1) * E, :] = grads[
                :, z * 128 : (z + 1) * 128
            ]

        def to_layers(e, carry):
            eg_ref[me, half, e] = mix_ref[pl.ds(half * count + e, 8, stride=E), :]
            return carry

        lax.fori_loop(0, E, to_layers, 0, unroll=E)

    beam_z, beam_y = me // 4, me % 4
    up = beam_z * 4 + (beam_y + 1) % 4
    down = beam_z * 4 + (beam_y + 3) % 4
    across = (1 - beam_z) * 4 + beam_y
    far_side = beam_z * 4 + (beam_y + 2) % 4
    across_up = (1 - beam_z) * 4 + (beam_y + 1) % 4
    across_down = (1 - beam_z) * 4 + (beam_y + 3) % 4
    across_far = (1 - beam_z) * 4 + (beam_y + 2) % 4

    eg_sends = []

    def hand(block, half, dst):
        copy = remote(
            eg_ref.at[block, half],
            eg_ref.at[block, half],
            eg_ss.at[len(eg_sends)],
            eg_rs.at[block, half],
            {"beam": dst},
        )
        copy.start()
        eg_sends.append(copy)

    def arrive(block, half):
        remote(
            eg_ref.at[block, half],
            eg_ref.at[block, half],
            eg_ss.at[0],
            eg_rs.at[block, half],
            {"beam": block},
        ).wait_recv()

    wait_u(0)
    own_half(0)
    hand(me, 0, up)
    hand(me, 0, across)
    hand(me, 0, down)
    wait_u(1)
    for step in range(1, NB):
        src = peer(step)
        remote(pr_src.at[src], pr_rcv.at[src], pr_ss.at[0], pr_rs.at[src], {"beam": src}).wait_recv()
    piece = pr_rcv[0]
    for d in range(1, NB):
        piece = piece + pr_rcv[d]
    pa_rcv[near] = piece
    pa_sends = []
    for step in range(1, n_near):
        copy = remote(
            pa_rcv.at[near], pa_rcv.at[near], pa_ss.at[step], pa_rs.at[near], near_id(step)
        )
        copy.start()
        pa_sends.append(copy)
    own_half(1)
    hand(me, 1, down)
    hand(me, 1, across)
    hand(me, 1, up)

    def weigh(e, sums):
        value = jnp.concatenate([eg_ref[me, 0, e], eg_ref[me, 1, e]], 0)
        return tuple(
            sums[d] + value * jnp.concatenate([u_rcv[d, 0, e], u_rcv[d, 1, e]], 0)
            for d in range(NB)
        )

    weighted = lax.fori_loop(0, E, weigh, (jnp.zeros((ZB, 128), F32),) * NB, unroll=8)

    for step in range(1, NB):
        src = peer(step)
        remote(tg_src.at[src], tg_rcv.at[src], tg_ss.at[0], tg_rs.at[src], {"beam": src}).wait_recv()
    tile_real = tg_rcv[0, 0]
    tile_imag = tg_rcv[0, 1]
    for d in range(1, NB):
        tile_real = tile_real + tg_rcv[d, 0]
        tile_imag = tile_imag + tg_rcv[d, 1]
    own_real, own_imag = ow_src[0, 0], ow_src[0, 1]
    grad_absorb = -object_weight * (own_real * tile_real + own_imag * tile_imag)
    grad_phase = object_weight * (own_real * tile_imag - own_imag * tile_real)
    later = jnp.zeros((ZB, 128), F32)
    for d in range(NB - 1, -1, -1):
        lg_src[d, 0] = later
        lg_src[d, 1] = grad_absorb
        lg_src[d, 2] = grad_phase
        later = later + weighted[d] * shield[d]
    lg_sends = []
    for step in range(1, NB):
        dst = peer(step)
        copy = remote(
            lg_src.at[dst], lg_rcv.at[me], lg_ss.at[step], lg_rs.at[me], {"beam": dst}
        )
        copy.start()
        lg_sends.append(copy)
    lg_rcv[me] = lg_src[me]

    def out_copy(order, block):
        return pltpu.make_async_copy(
            out_v.at[:, block], out_hbm.at[:, block], out_sem.at[order]
        )

    def finish(order, block):
        def grad_of(e):
            return jnp.concatenate([eg_ref[block, 0, e], eg_ref[block, 1, e]], 0)

        def weigh_cells(e, sums):
            value = grad_of(e)
            return tuple(sums[x] + value * cell(e, block, x) for x in range(X))

        zero = jnp.zeros((ZB, 128), F32)
        sums = lax.fori_loop(0, E, weigh_cells, (zero,) * X, unroll=E)
        light = [inc_ref[block, x] for x in range(X)]
        beyond = [None] * X
        running = lg_rcv[block, 0]
        for x in range(X - 1, -1, -1):
            beyond[x] = running
            running = running + light[x] * sums[x]
        absorb_grad, phase_grad = lg_rcv[block, 1], lg_rcv[block, 2]

        def write(e, carry):
            value = grad_of(e)
            shared = beta_ref[e] * absorb_grad + delta_ref[e] * phase_grad
            for x in range(X):
                result = value * light[x] - atten_ref[e] * beyond[x] + shared
                dens_f[e, block, pl.ds(x, ZB, stride=X), :] = result
            out_v[e, block] = dens_f[e, block].astype(BF16)
            return carry

        lax.fori_loop(0, E, write, 0, unroll=E)
        out_copy(order, block).start()

    def extras(block):
        remote(lg_src.at[block], lg_rcv.at[block], lg_ss.at[0], lg_rs.at[block], {"beam": block}).wait_recv()

    arrive(down, 0)
    hand(down, 0, up)
    arrive(across, 0)
    hand(across, 0, up)
    hand(across, 0, down)
    arrive(up, 1)
    hand(up, 1, down)
    arrive(across, 1)
    hand(across, 1, up)
    hand(across, 1, down)
    finish(0, me)

    for step in range(1, n_near):
        src = (near + step) % n_near
        remote(pa_rcv.at[src], pa_rcv.at[src], pa_ss.at[0], pa_rs.at[src], near_id(step)).wait_recv()
    piece = pa_rcv[0]
    for d in range(1, n_near):
        piece = piece + pa_rcv[d]
    pb_rcv[row_x] = piece
    pb_sends = []
    for step in range(1, n_x):
        copy = remote(
            pb_rcv.at[row_x], pb_rcv.at[row_x], pb_ss.at[step], pb_rs.at[row_x], x_id(step)
        )
        copy.start()
        pb_sends.append(copy)

    arrive(down, 1)
    extras(down)
    finish(1, down)
    arrive(far_side, 0)
    hand(far_side, 0, across)
    arrive(far_side, 1)
    hand(far_side, 1, across)
    arrive(up, 0)
    extras(up)
    finish(2, up)
    extras(across)
    finish(3, across)

    for step in range(1, n_x):
        src = (row_x + step) % n_x
        remote(pb_rcv.at[src], pb_rcv.at[src], pb_ss.at[0], pb_rs.at[src], x_id(step)).wait_recv()
    piece = pb_rcv[0]
    for d in range(1, n_x):
        piece = piece + pb_rcv[d]
    pf_rcv[me] = piece * (1.0 / total)
    pf_sends = []
    for step in range(1, NB):
        copy = remote(
            pf_rcv.at[me], pf_rcv.at[me], pf_ss.at[step], pf_rs.at[me], {"beam": peer(step)}
        )
        copy.start()
        pf_sends.append(copy)

    extras(far_side)
    finish(4, far_side)
    arrive(across_up, 0)
    arrive(across_up, 1)
    extras(across_up)
    finish(5, across_up)
    arrive(across_down, 0)
    arrive(across_down, 1)
    extras(across_down)
    finish(6, across_down)
    for step in range(1, NB):
        src = peer(step)
        remote(pf_rcv.at[src], pf_rcv.at[src], pf_ss.at[0], pf_rs.at[src], {"beam": src}).wait_recv()
    for d in range(NB):
        for g in range(8):
            start = (d % 4 * 8 + g) * 128
            probe_out[d // 4 : d // 4 + 1, start : start + 128] = pf_rcv[d, g : g + 1, :]
    arrive(across_far, 0)
    arrive(across_far, 1)
    extras(across_far)
    finish(7, across_far)

    for copy in tap_sends + u_sends + ow_sends + tg_sends + pr_sends + pa_sends + eg_sends + lg_sends + pb_sends + pf_sends:
        copy.wait_send()
    for order, block in enumerate(
        [me, down, up, across, far_side, across_up, across_down, across_far]
    ):
        out_copy(order, block).wait()


def hand_over(grad_hbm, probe_hbm, grad_out, probe_out, grad_v, probe_v, in_sems, out_sems):
    count = E // PART
    loads, stores = [], []
    for part in range(count):
        rows = pl.ds(part * PART, PART)
        loads.append(
            pltpu.make_async_copy(grad_hbm.at[rows], grad_v.at[rows], in_sems.at[part])
        )
        stores.append(
            pltpu.make_async_copy(grad_v.at[rows], grad_out.at[rows], out_sems.at[part])
        )
    loads.append(pltpu.make_async_copy(probe_hbm, probe_v, in_sems.at[count]))
    stores.append(pltpu.make_async_copy(probe_v, probe_out, out_sems.at[count]))
    for load in loads:
        load.start()
    for load, store in zip(loads, stores):
        load.wait()
        store.start()
    for store in stores:
        store.wait()


def body(
    sizes,
    densities,
    spectra,
    intensities,
    positions,
    probe,
    line_channels,
    line_weights,
    atten_coef,
    beta_coef,
    delta_coef,
):
    n_grp, n_row, n_x, n_zh, total = sizes
    chirps, right, left = constant_tables()
    dens = densities.reshape(E, NB, ZB * X, 128)
    spec = spectra.reshape(ZB * 128, C)
    vmem = pl.BlockSpec(memory_space=pltpu.VMEM)
    smem = pl.BlockSpec(memory_space=pltpu.SMEM)
    anywhere = pl.BlockSpec(memory_space=pl.ANY)
    n_near = n_grp * n_zh
    dma = pltpu.SemaphoreType.DMA
    small = (NB, 3, ZB, 128)
    out, probe_grad = pl.pallas_call(
        functools.partial(kernel, sizes),
        out_shape=(
            jax.ShapeDtypeStruct((E, NB, ZB * X, 128), BF16),
            jax.ShapeDtypeStruct((2, M * M), F32),
        ),
        in_specs=[
            anywhere,
            anywhere,
            anywhere,
            smem,
            vmem,
            vmem,
            vmem,
            smem,
            smem,
            smem,
            vmem,
            vmem,
            vmem,
        ],
        out_specs=(anywhere, vmem),
        scratch_shapes=[
            pltpu.VMEM((E, NB, ZB * X, 128), BF16),
            pltpu.VMEM((E, NB, ZB * X, 128), F32),
            pltpu.VMEM((ZB * 128, C), BF16),
            pltpu.VMEM((K, M * M), BF16),
            pltpu.VMEM((K * M, 128), F32),
            pltpu.VMEM((2, M, 128), F32),
            pltpu.VMEM(small, F32),
            pltpu.VMEM(small, F32),
            pltpu.VMEM((NB, 2, E, 8, 128), F32),
            pltpu.VMEM((NB, 2, E, 8, 128), F32),
            pltpu.VMEM(small, F32),
            pltpu.VMEM(small, F32),
            pltpu.VMEM((NB, X, ZB, 128), F32),
            pltpu.VMEM((NB, 2, ZB, 128), F32),
            pltpu.VMEM((NB, 2, ZB, 128), F32),
            pltpu.VMEM(small, F32),
            pltpu.VMEM(small, F32),
            pltpu.VMEM((NB, 2, E, 8, 128), F32),
            pltpu.VMEM((ZB * E, 128), F32),
            pltpu.VMEM((E, ZB * 128), F32),
            pltpu.VMEM((E, NB, ZB * X, 128), BF16),
            pltpu.VMEM((128, 256), F32),
            pltpu.VMEM((2, M, 128), F32),
            pltpu.VMEM((NB, 8, 128), F32),
            pltpu.VMEM((NB, 8, 128), F32),
            pltpu.VMEM((n_near, 8, 128), F32),
            pltpu.VMEM((n_x, 8, 128), F32),
            pltpu.VMEM((NB, 8, 128), F32),
            dma((NB,)),
            dma,
            dma,
            dma((NB,)),
            dma((NB,)),
            dma((NB,)),
            dma((NB, 2)),
            dma((NB, 2)),
            dma((NB,)),
            dma((NB,)),
            dma((NB,)),
            dma((NB,)),
            dma((NB,)),
            dma((NB,)),
            dma((14,)),
            dma((NB, 2)),
            dma((NB,)),
            dma((NB,)),
            dma((n_near,)),
            dma((n_near,)),
            dma((n_x,)),
            dma((n_x,)),
            dma((NB,)),
            dma((NB,)),
        ],
        compiler_params=pltpu.CompilerParams(
            collective_id=0, has_side_effects=True, vmem_limit_bytes=60 * 1024 * 1024
        ),
    )(
        dens,
        spec,
        intensities,
        positions.T,
        probe,
        line_channels.T,
        line_weights.T,
        atten_coef,
        beta_coef,
        delta_coef,
        jnp.asarray(chirps),
        jnp.asarray(right),
        jnp.asarray(left),
    )
    out, probe_grad = pl.pallas_call(
        hand_over,
        out_shape=(
            jax.ShapeDtypeStruct(out.shape, BF16),
            jax.ShapeDtypeStruct(probe_grad.shape, F32),
        ),
        in_specs=[anywhere, anywhere],
        out_specs=(anywhere, anywhere),
        scratch_shapes=[
            pltpu.VMEM(out.shape, BF16),
            pltpu.VMEM(probe_grad.shape, F32),
            dma((E // PART + 1,)),
            dma((E // PART + 1,)),
        ],
        compiler_params=pltpu.CompilerParams(vmem_limit_bytes=60 * 1024 * 1024),
    )(out, probe_grad)
    return out.reshape(densities.shape), probe_grad


def solution(mesh):
    n_grp, n_beam, n_row = mesh.shape["grp"], mesh.shape["beam"], mesh.shape["row"]
    n_zh = 4 if n_row % 4 == 0 else 1
    sizes = (n_grp, n_row, n_row // n_zh, n_zh, float(K * n_grp * n_beam * n_row))
    return jax.shard_map(
        functools.partial(body, sizes),
        mesh=mesh,
        in_specs=(
            P(None, "grp", "beam", "row"),
            P(("grp", "beam"), "row", None),
            P(("grp", "beam", "row"), None),
            P(("grp", "beam", "row"), None),
            P(),
            P(),
            P(),
            P(),
            P(),
            P(),
        ),
        out_specs=(P(None, "grp", "beam", "row"), P()),
        check_vma=False,
    )
```

```python
import functools
import math

import jax
import jax.numpy as jnp
import numpy as np
from jax import lax
from jax.experimental import pallas as pl
from jax.experimental.pallas import tpu as pltpu
from jax.sharding import PartitionSpec as P

E = 32
C = 512
M = 64
K = 32
X = 4
ZB = 16
NB = 8
GROUP = 16
NEAREST = (4, 1, 7, 3, 5, 2, 6)
ORDER = tuple((step, half) for half in range(2) for step in NEAREST)
EARLY = 7
PART = 4

F32 = jnp.float32
BF16 = jnp.bfloat16
HIGHEST = lax.Precision.HIGHEST
MESH = pl.DeviceIdType.MESH
object_weight = 1000.0


def halves(values):
    high = values.astype(BF16)
    return high, (values - high.astype(F32)).astype(BF16)


def swap(values):
    return pltpu.roll(values, M, 1)


def matmul(left, right):
    return jnp.dot(left, right, preferred_element_type=F32)


def np_halves(values):
    high = values.astype(np.float32).astype(jnp.bfloat16)
    low = (values - high.astype(np.float64)).astype(np.float32).astype(jnp.bfloat16)
    return high, low


def constant_tables():
    index = np.arange(M)
    angles = 2.0 * math.pi / M * (index[:, None] * index[None, :] % M)
    dft_real = np.cos(angles) / math.sqrt(M)
    dft_imag = -np.sin(angles) / math.sqrt(M)
    centred = np.arange(M) - M // 2
    chirp = math.pi * 0.5 / M * (centred[:, None] ** 2 + centred[None, :] ** 2)
    chirp_real, chirp_imag = np.cos(chirp), np.sin(chirp)
    chirps = np.stack(
        [
            np.concatenate([chirp_real, chirp_real], 1),
            np.concatenate([-chirp_imag, chirp_imag], 1),
        ]
    ).astype(np.float32)

    def right_table(sign):
        table = np.block([[dft_real, sign * dft_imag], [-sign * dft_imag, dft_real]])
        high, low = np_halves(table)
        row = np.concatenate([high, low], 1)
        return np.concatenate([row, row], 0)

    right = np.stack([right_table(1.0), right_table(-1.0)])
    high, low = np_halves(np.concatenate([dft_real, dft_imag], 0))
    left = np.concatenate([high, high, low, low], 1)
    return chirps, right, left


def kernel(
    sizes,
    dens_hbm,
    spec_hbm,
    inten_hbm,
    pos_ref,
    probe_ref,
    chan_ref,
    weight_ref,
    atten_ref,
    beta_ref,
    delta_ref,
    chirp_ref,
    right_ref,
    left_ref,
    out_hbm,
    probe_out,
    dens_bf,
    dens_f,
    spec_v,
    inten_bf,
    inten_f,
    image_ref,
    tap_src,
    tap_rcv,
    u_src,
    u_rcv,
    ow_src,
    ow_rcv,
    inc_ref,
    tg_src,
    tg_rcv,
    lg_src,
    lg_rcv,
    eg_ref,
    mix_ref,
    fit_ref,
    out_v,
    tile_ref,
    pgsum_ref,
    pr_src,
    pr_rcv,
    pa_rcv,
    pb_rcv,
    pf_rcv,
    dens_sem,
    spec_sem,
    inten_sem,
    out_sem,
    tap_ss,
    tap_rs,
    u_ss,
    u_rs,
    ow_ss,
    ow_rs,
    tg_ss,
    tg_rs,
    lg_ss,
    lg_rs,
    eg_ss,
    eg_rs,
    pr_ss,
    pr_rs,
    pa_ss,
    pa_rs,
    pb_ss,
    pb_rs,
    pf_ss,
    pf_rs,
    hello_sem,
):
    n_grp, n_row, n_x, n_zh, total = sizes
    me = lax.axis_index("beam")
    grp = lax.axis_index("grp")
    row = lax.axis_index("row")
    row_x, row_z = row // n_zh, row % n_zh
    n_near = n_grp * n_zh
    near = grp * n_zh + row_z

    def near_id(step):
        other = (near + step) % n_near
        return {"grp": other // n_zh, "row": row_x * n_zh + other % n_zh}

    def x_id(step):
        return {"row": ((row_x + step) % n_x) * n_zh + row_z}

    def peer(step):
        return (me + step) % NB

    def remote(source, target, send, recv, device):
        return pltpu.make_async_remote_copy(
            src_ref=source,
            dst_ref=target,
            send_sem=send,
            recv_sem=recv,
            device_id=device,
            device_id_type=MESH,
        )

    barrier = pltpu.get_barrier_semaphore()
    is_lead = me == 0
    for step in range(1, NB):
        dst = peer(step)

        @pl.when(dst != 0)
        def _():
            pl.semaphore_signal(barrier, inc=1, device_id={"beam": dst}, device_id_type=MESH)

    @pl.when(is_lead)
    def _():
        for step in range(1, n_near):
            pl.semaphore_signal(barrier, inc=1, device_id=near_id(step), device_id_type=MESH)
        for step in range(1, n_x):
            pl.semaphore_signal(barrier, inc=1, device_id=x_id(step), device_id_type=MESH)

    def dens_copy(step):
        block = (me + 1 + step) % NB
        return pltpu.make_async_copy(
            dens_hbm.at[:, block], dens_bf.at[:, block], dens_sem.at[step]
        )

    for step in range(NB):
        dens_copy(step).start()
    spec_copy = pltpu.make_async_copy(spec_hbm, spec_v, spec_sem)
    spec_copy.start()
    inten_copy = pltpu.make_async_copy(inten_hbm, inten_bf, inten_sem)
    inten_copy.start()

    def cell(e, block, x):
        return dens_f[e, block, pl.ds(x, ZB, stride=X), :]

    def project(step, carry):
        block = (me + 1 + step) % NB
        dens_copy(step).wait()
        dens_f[:, block] = dens_bf[:, block].astype(F32)

        def add(e, sums):
            cells = [cell(e, block, x) for x in range(X)]
            total_cells = (cells[0] + cells[1]) + (cells[2] + cells[3])
            optical = [sums[x] + atten_ref[e] * cells[x] for x in range(X)]
            return (
                *optical,
                sums[X] + beta_ref[e] * total_cells,
                sums[X + 1] + delta_ref[e] * total_cells,
            )

        zero = jnp.zeros((ZB, 128), F32)
        sums = lax.fori_loop(0, E, add, (zero,) * (X + 2), unroll=E)
        depth = zero
        for x in range(X):
            inc_ref[block, x] = jnp.exp(-depth)
            depth = depth + sums[x]
        tap_src[block, 0] = depth
        tap_src[block, 1] = sums[X]
        tap_src[block, 2] = sums[X + 1]

        return carry

    lax.fori_loop(0, NB, project, 0)
    @pl.when(jnp.logical_not(is_lead))
    def _():
        pl.semaphore_wait(barrier, NB - 1)
        pl.semaphore_signal(hello_sem, inc=1, device_id={"beam": 0}, device_id_type=MESH)

    @pl.when(is_lead)
    def _():
        pl.semaphore_wait(hello_sem, NB - 1)

    tap_sends, u_sends = [], []

    def send_tap(step):
        dst = peer(step)
        copy = remote(
            tap_src.at[dst], tap_rcv.at[me], tap_ss.at[step], tap_rs.at[me], {"beam": dst}
        )
        copy.start()
        tap_sends.append(copy)

    def u_copy(step, half):
        dst = peer(step)
        return remote(
            u_src.at[dst, half],
            u_rcv.at[me, half],
            u_ss.at[step, half],
            u_rs.at[me, half],
            {"beam": dst},
        )

    def send_u(step, half):
        copy = u_copy(step, half)
        copy.start()
        u_sends.append(copy)

    def wait_u(half):
        for step in range(1, NB):
            src = peer(step)
            remote(
                u_src.at[src, half],
                u_rcv.at[src, half],
                u_ss.at[step, half],
                u_rs.at[src, half],
                {"beam": src},
            ).wait_recv()

    for step in range(1, NB):
        send_tap(step)
    tap_rcv[me] = tap_src[me]

    def emit(step, carry):
        block = (me + 1 + step) % NB
        local = [inc_ref[block, x] for x in range(X)]

        def one(e, inner):
            terms = [cell(e, block, x) * local[x] for x in range(1, X)]
            value = (cell(e, block, 0) + terms[0]) + (terms[1] + terms[2])
            u_src[block, 0, e] = value[:8]
            u_src[block, 1, e] = value[8:]
            return inner

        lax.fori_loop(0, E, one, 0, unroll=E)

        return carry

    lax.fori_loop(0, NB, emit, 0)
    for step, half in ORDER[:EARLY]:
        send_u(step, half)
    u_rcv[me] = u_src[me]

    for step in range(1, NB):
        src = peer(step)
        remote(tap_src.at[src], tap_rcv.at[src], tap_ss.at[0], tap_rs.at[src], {"beam": src}).wait_recv()
    before = jnp.zeros((ZB, 128), F32)
    absorb = jnp.zeros((ZB, 128), F32)
    phase = jnp.zeros((ZB, 128), F32)
    for d in range(NB):
        ow_src[d, 2] = jnp.exp(-before)
        before = before + tap_rcv[d, 0]
        absorb = absorb + tap_rcv[d, 1]
        phase = phase + tap_rcv[d, 2]
    amplitude = jnp.exp(-absorb)
    own_real = amplitude * jnp.cos(phase)
    own_imag = amplitude * jnp.sin(phase)
    for d in range(NB):
        ow_src[d, 0] = own_real
        ow_src[d, 1] = own_imag
    ow_sends = []
    for step in range(1, NB):
        dst = peer(step)
        copy = remote(
            ow_src.at[dst], ow_rcv.at[me], ow_ss.at[step], ow_rs.at[me], {"beam": dst}
        )
        copy.start()
        ow_sends.append(copy)
    ow_rcv[me] = ow_src[me]
    for step, half in ORDER[EARLY:]:
        send_u(step, half)

    eye = (
        lax.broadcasted_iota(jnp.int32, (E, E), 0) == lax.broadcasted_iota(jnp.int32, (E, E), 1)
    ).astype(F32)

    def columns_of(rows):
        return lax.dot_general(
            eye, rows, (((1,), (1,)), ((), ())), precision=HIGHEST, preferred_element_type=F32
        )

    lines = columns_of(chan_ref[...].astype(F32))
    strengths = columns_of(weight_ref[...])
    channel = lax.broadcasted_iota(jnp.int32, (E, C), 1).astype(F32)
    table = jnp.zeros((E, C), F32)
    for line in range(4):
        offset = channel - lines[:, line : line + 1]
        table = table + strengths[:, line : line + 1] * jnp.exp(-offset * offset / 8.0)
    gram = lax.dot_general(
        table, table, (((1,), (1,)), ((), ())), precision=HIGHEST, preferred_element_type=F32
    )
    gram_high, gram_low = halves(gram)
    gram_parts = jnp.concatenate([gram_high, gram_low], 0)

    spec_copy.wait()
    table_high, table_low = halves(table)
    fit = lax.dot_general(
        jnp.concatenate([table_high, table_low], 0),
        spec_v[...],
        (((1,), (1,)), ((), ())),
        preferred_element_type=F32,
    )
    fit_ref[...] = fit[:E] + fit[E:]

    lane = lax.broadcasted_iota(jnp.int32, (M, 128), 1)
    first = lane < M
    even = lax.broadcasted_iota(jnp.int32, (M, 128), 0) % 2 == 0
    inten_copy.wait()
    flat = inten_bf[...].astype(F32)
    for g in range(M // 2):
        group = flat[:, g * 128 : (g + 1) * 128]
        inten_f[pl.ds(2 * g, K, stride=M), :] = group
        inten_f[pl.ds(2 * g + 1, K, stride=M), :] = group
    for part in range(2):
        for g in range(M // 2):
            group = probe_ref[part : part + 1, g * 128 : (g + 1) * 128]
            image_ref[part, 2 * g : 2 * g + 1, :] = group
            image_ref[part, 2 * g + 1 : 2 * g + 2, :] = group
    image_real, image_imag = image_ref[0], image_ref[1]
    probe = jnp.where(
        first,
        jnp.where(even, image_real, swap(image_real)),
        jnp.where(even, swap(image_imag), image_imag),
    )
    keep = first == even

    for step in range(1, NB):
        src = peer(step)
        remote(ow_src.at[src], ow_rcv.at[src], ow_ss.at[0], ow_rs.at[src], {"beam": src}).wait_recv()

    illum = probe * chirp_ref[0] + swap(probe) * chirp_ref[1]
    illum_swap = swap(illum)
    illum_a = jnp.where(first, illum, illum_swap)
    illum_b = jnp.where(first, -illum_swap, illum)
    sign = jnp.where(first, -1.0, 1.0).astype(F32)

    obj_real = ow_rcv[:, 0].reshape(NB * ZB, 128)
    obj_imag = ow_rcv[:, 1].reshape(NB * ZB, 128)
    real_high, real_low = halves(obj_real)
    imag_high, imag_low = halves(obj_imag)
    field = jnp.concatenate([real_high, imag_high, real_low, imag_low], 1)

    pick_z = lax.broadcasted_iota(jnp.int32, (M, 128), 1) - lax.broadcasted_iota(
        jnp.int32, (M, 128), 0
    )
    gather_row = lax.broadcasted_iota(jnp.int32, (256, 128), 0)
    gather_col = lax.broadcasted_iota(jnp.int32, (256, 128), 1)
    pick_y = jnp.where(
        (gather_row < 128) == (gather_col < M), gather_row % 128 - gather_col % M, -1
    )
    spread_row = lax.broadcasted_iota(jnp.int32, (128, 256), 0)
    spread_col = lax.broadcasted_iota(jnp.int32, (128, 256), 1)
    place_y = jnp.where(
        (spread_col < 128) == (spread_row < M), spread_col % 128 - spread_row % M, -1
    )
    place_z = lax.broadcasted_iota(jnp.int32, (128, 128), 0) - (
        lax.broadcasted_iota(jnp.int32, (128, 128), 1) % M
    )

    tile_ref[...] = jnp.zeros(tile_ref.shape, F32)
    pgsum_ref[...] = jnp.zeros(pgsum_ref.shape, F32)

    def transform(values, right, conj):
        high, low = halves(values)
        product = matmul(jnp.concatenate([high, low], 1), right)
        product = product[:, :128] + product[:, 128:]
        high, low = halves(product)
        outs = []
        for i in range(GROUP):
            part = slice(i * M, (i + 1) * M)
            stack = jnp.concatenate([high[part], low[part], high[part], low[part]], 0)
            both = matmul(left_ref[...], stack)
            turned = swap(both[M:]) * sign
            outs.append(both[:M] - turned if conj else both[:M] + turned)
        return outs

    def positions_step(group, carry):
        windows, picks = [], []
        starts = [
            (pos_ref[0, group * GROUP + i], pos_ref[1, group * GROUP + i])
            for i in range(GROUP)
        ]
        for i in range(GROUP):
            rows = (pick_z == starts[i][0]).astype(F32).astype(BF16)
            cut = matmul(rows, field).astype(BF16)
            stack = jnp.concatenate([cut[:, :256], cut[:, 256:]], 0)
            columns = (pick_y == starts[i][1]).astype(F32).astype(BF16)
            both = matmul(stack, columns)
            windows.append(both[:M] + both[M:])
        exits = [w * illum_a + swap(w) * illum_b for w in windows]
        far = transform(jnp.concatenate(exits, 0), right_ref[0], False)
        pulled = []
        for i in range(GROUP):
            square = far[i] * far[i]
            start = pl.multiple_of((group * GROUP + i) * M, M)
            measured = inten_f[pl.ds(start, M), :]
            measured = jnp.where(keep, measured, swap(measured))
            misfit = square + swap(square) - measured
            pulled.append(misfit * far[i])
        back = transform(jnp.concatenate(pulled, 0), right_ref[1], True)
        sum_a = pgsum_ref[0]
        sum_b = pgsum_ref[1]
        tile = tile_ref[...]
        for i in range(GROUP):
            sum_a = sum_a + windows[i] * back[i]
            sum_b = sum_b + swap(windows[i]) * back[i]
            grad = back[i] * illum_a - swap(back[i]) * illum_b
            high, low = halves(grad)
            columns = (place_y == starts[i][1]).astype(F32).astype(BF16)
            spread = matmul(jnp.concatenate([high, low], 0), columns).astype(BF16)
            rows = (place_z == starts[i][0]).astype(F32).astype(BF16)
            tile = tile + matmul(rows, spread)
        pgsum_ref[0] = sum_a
        pgsum_ref[1] = sum_b
        tile_ref[...] = tile
        return carry

    lax.fori_loop(0, K // GROUP, positions_step, 0)

    for d in range(NB):
        tg_src[d, 0] = tile_ref[d * ZB : (d + 1) * ZB, :128]
        tg_src[d, 1] = tile_ref[d * ZB : (d + 1) * ZB, 128:]
    sum_a, sum_b = pgsum_ref[0], pgsum_ref[1]
    conj_sum = jnp.where(first, sum_a + swap(sum_a), sum_b - swap(sum_b))
    local_probe = conj_sum * chirp_ref[0] - swap(conj_sum) * chirp_ref[1]
    image_ref[0] = local_probe
    upper, lower = image_ref[0, pl.ds(0, M // 2, stride=2), :], image_ref[0, pl.ds(1, M // 2, stride=2), :]
    half_first = first[: M // 2]
    flat_real = jnp.where(half_first, upper, swap(lower))
    flat_imag = jnp.where(half_first, swap(upper), lower)
    pr_src[: M // 2] = flat_real
    pr_src[M // 2 :] = flat_imag
    tg_sends = []
    for step in range(1, NB):
        dst = peer(step)
        copy = remote(
            tg_src.at[dst], tg_rcv.at[me], tg_ss.at[step], tg_rs.at[me], {"beam": dst}
        )
        copy.start()
        tg_sends.append(copy)

    def pr_copy(src):
        return remote(pr_src, pr_rcv.at[src], pr_ss, pr_rs.at[src], {"beam": 0})

    @pl.when(jnp.logical_not(is_lead))
    def _():
        pr_copy(me).start()

    tg_rcv[me] = tg_src[me]

    def scale_block(block, carry):
        for x in range(X):
            inc_ref[block, x] = inc_ref[block, x] * ow_rcv[block, 2]
        return carry

    lax.fori_loop(0, NB, scale_block, 0)

    shield = [ow_src[d, 2] for d in range(NB)]

    def own_half(half):
        rows = slice(half * 8, half * 8 + 8)
        count = E * 8

        def add_slabs(e, carry):
            value = u_rcv[0, half, e] * shield[0][rows]
            for d in range(1, NB):
                value = value + u_rcv[d, half, e] * shield[d][rows]
            mix_ref[pl.ds(half * count + e, 8, stride=E), :] = value
            return carry

        lax.fori_loop(0, E, add_slabs, 0, unroll=E)
        columns = jnp.concatenate(
            [mix_ref[half * count + z * E : half * count + (z + 1) * E, :] for z in range(8)], 1
        )
        high, low = halves(columns)
        product = matmul(gram_parts, jnp.concatenate([high, low], 1))
        product = product[:E] + product[E:]
        grads = (product[:, :1024] + product[:, 1024:]) - fit_ref[:, half * 1024 : half * 1024 + 1024]
        for z in range(8):
            mix_ref[half * count + z * E : half * count + (z + 1) * E, :] = grads[
                :, z * 128 : (z + 1) * 128
            ]

        def to_layers(e, carry):
            eg_ref[me, half, e] = mix_ref[pl.ds(half * count + e, 8, stride=E), :]
            return carry

        lax.fori_loop(0, E, to_layers, 0, unroll=E)

    beam_z, beam_y = me // 4, me % 4
    up = beam_z * 4 + (beam_y + 1) % 4
    down = beam_z * 4 + (beam_y + 3) % 4
    across = (1 - beam_z) * 4 + beam_y
    far_side = beam_z * 4 + (beam_y + 2) % 4
    across_up = (1 - beam_z) * 4 + (beam_y + 1) % 4
    across_down = (1 - beam_z) * 4 + (beam_y + 3) % 4
    across_far = (1 - beam_z) * 4 + (beam_y + 2) % 4

    eg_sends = []

    def hand(block, half, dst):
        copy = remote(
            eg_ref.at[block, half],
            eg_ref.at[block, half],
            eg_ss.at[len(eg_sends)],
            eg_rs.at[block, half],
            {"beam": dst},
        )
        copy.start()
        eg_sends.append(copy)

    def arrive(block, half):
        remote(
            eg_ref.at[block, half],
            eg_ref.at[block, half],
            eg_ss.at[0],
            eg_rs.at[block, half],
            {"beam": block},
        ).wait_recv()

    wait_u(0)
    own_half(0)
    hand(me, 0, up)
    hand(me, 0, across)
    hand(me, 0, down)
    wait_u(1)

    def pa_copy(step, owner):
        return remote(
            pa_rcv.at[owner], pa_rcv.at[owner], pa_ss.at[step], pa_rs.at[owner], near_id(step)
        )

    def pb_copy(step, owner):
        return remote(
            pb_rcv.at[owner], pb_rcv.at[owner], pb_ss.at[step], pb_rs.at[owner], x_id(step)
        )

    def pf_copy(step):
        return remote(pf_rcv, pf_rcv, pf_ss.at[step], pf_rs, {"beam": peer(step)})

    @pl.when(is_lead)
    def _():
        for src in range(1, NB):
            pr_copy(src).wait_recv()
        piece = pr_src[...]
        for src in range(1, NB):
            piece = piece + pr_rcv[src]
        pa_rcv[near] = piece
        pl.semaphore_wait(barrier, n_near - 1 + n_x - 1)
        for step in range(1, n_near):
            pa_copy(step, near).start()

    own_half(1)
    hand(me, 1, down)
    hand(me, 1, across)
    hand(me, 1, up)

    def weigh(e, sums):
        value = jnp.concatenate([eg_ref[me, 0, e], eg_ref[me, 1, e]], 0)
        return tuple(
            sums[d] + value * jnp.concatenate([u_rcv[d, 0, e], u_rcv[d, 1, e]], 0)
            for d in range(NB)
        )

    weighted = lax.fori_loop(0, E, weigh, (jnp.zeros((ZB, 128), F32),) * NB, unroll=8)

    for step in range(1, NB):
        src = peer(step)
        remote(tg_src.at[src], tg_rcv.at[src], tg_ss.at[0], tg_rs.at[src], {"beam": src}).wait_recv()
    tile_real = tg_rcv[0, 0]
    tile_imag = tg_rcv[0, 1]
    for d in range(1, NB):
        tile_real = tile_real + tg_rcv[d, 0]
        tile_imag = tile_imag + tg_rcv[d, 1]
    own_real, own_imag = ow_src[0, 0], ow_src[0, 1]
    grad_absorb = -object_weight * (own_real * tile_real + own_imag * tile_imag)
    grad_phase = object_weight * (own_real * tile_imag - own_imag * tile_real)
    later = jnp.zeros((ZB, 128), F32)
    for d in range(NB - 1, -1, -1):
        lg_src[d, 0] = later
        lg_src[d, 1] = grad_absorb
        lg_src[d, 2] = grad_phase
        later = later + weighted[d] * shield[d]
    lg_sends = []
    for step in range(1, NB):
        dst = peer(step)
        copy = remote(
            lg_src.at[dst], lg_rcv.at[me], lg_ss.at[step], lg_rs.at[me], {"beam": dst}
        )
        copy.start()
        lg_sends.append(copy)
    lg_rcv[me] = lg_src[me]

    def out_copy(order, block):
        return pltpu.make_async_copy(
            out_v.at[:, block], out_hbm.at[:, block], out_sem.at[order]
        )

    def finish(order, block):
        def grad_of(e):
            return jnp.concatenate([eg_ref[block, 0, e], eg_ref[block, 1, e]], 0)

        def weigh_cells(e, sums):
            value = grad_of(e)
            return tuple(sums[x] + value * cell(e, block, x) for x in range(X))

        zero = jnp.zeros((ZB, 128), F32)
        sums = lax.fori_loop(0, E, weigh_cells, (zero,) * X, unroll=E)
        light = [inc_ref[block, x] for x in range(X)]
        beyond = [None] * X
        running = lg_rcv[block, 0]
        for x in range(X - 1, -1, -1):
            beyond[x] = running
            running = running + light[x] * sums[x]
        absorb_grad, phase_grad = lg_rcv[block, 1], lg_rcv[block, 2]

        def write(e, carry):
            value = grad_of(e)
            shared = beta_ref[e] * absorb_grad + delta_ref[e] * phase_grad
            for x in range(X):
                result = value * light[x] - atten_ref[e] * beyond[x] + shared
                dens_f[e, block, pl.ds(x, ZB, stride=X), :] = result
            out_v[e, block] = dens_f[e, block].astype(BF16)
            return carry

        lax.fori_loop(0, E, write, 0, unroll=E)
        out_copy(order, block).start()

    def extras(block):
        remote(lg_src.at[block], lg_rcv.at[block], lg_ss.at[0], lg_rs.at[block], {"beam": block}).wait_recv()

    arrive(down, 0)
    hand(down, 0, up)
    arrive(across, 0)
    hand(across, 0, up)
    hand(across, 0, down)
    arrive(up, 1)
    hand(up, 1, down)
    arrive(across, 1)
    hand(across, 1, up)
    hand(across, 1, down)
    finish(0, me)

    arrive(down, 1)
    extras(down)
    finish(1, down)
    arrive(far_side, 0)
    hand(far_side, 0, across)
    arrive(far_side, 1)
    hand(far_side, 1, across)

    @pl.when(is_lead)
    def _():
        for step in range(1, n_near):
            pa_copy(step, (near + step) % n_near).wait_recv()
        piece = pa_rcv[0]
        for d in range(1, n_near):
            piece = piece + pa_rcv[d]
        pb_rcv[row_x] = piece
        for step in range(1, n_x):
            pb_copy(step, row_x).start()

    arrive(up, 0)
    extras(up)
    finish(2, up)
    extras(across)
    finish(3, across)

    extras(far_side)
    finish(4, far_side)

    @pl.when(is_lead)
    def _():
        for step in range(1, n_x):
            pb_copy(step, (row_x + step) % n_x).wait_recv()
        piece = pb_rcv[0]
        for d in range(1, n_x):
            piece = piece + pb_rcv[d]
        pf_rcv[...] = piece * (1.0 / total)
        for step in range(1, NB):
            pf_copy(step).start()

    arrive(across_up, 0)
    arrive(across_up, 1)
    extras(across_up)
    finish(5, across_up)
    arrive(across_down, 0)
    arrive(across_down, 1)
    extras(across_down)
    finish(6, across_down)

    arrive(across_far, 0)
    arrive(across_far, 1)
    extras(across_far)
    finish(7, across_far)

    @pl.when(jnp.logical_not(is_lead))
    def _():
        pf_copy(1).wait_recv()

    for part in range(2):
        for g in range(M // 2):
            row_at = part * (M // 2) + g
            probe_out[part : part + 1, g * 128 : (g + 1) * 128] = pf_rcv[row_at : row_at + 1, :]

    for copy in tap_sends + u_sends + ow_sends + tg_sends + eg_sends + lg_sends:
        copy.wait_send()

    @pl.when(jnp.logical_not(is_lead))
    def _():
        pr_copy(me).wait_send()

    @pl.when(is_lead)
    def _():
        for step in range(1, n_near):
            pa_copy(step, near).wait_send()
        for step in range(1, n_x):
            pb_copy(step, row_x).wait_send()
        for step in range(1, NB):
            pf_copy(step).wait_send()

    for order, block in enumerate(
        [me, down, up, across, far_side, across_up, across_down, across_far]
    ):
        out_copy(order, block).wait()


def hand_over(grad_hbm, probe_hbm, grad_out, probe_out, grad_v, probe_v, in_sems, out_sems):
    count = E // PART
    loads, stores = [], []
    for part in range(count):
        rows = pl.ds(part * PART, PART)
        loads.append(
            pltpu.make_async_copy(grad_hbm.at[rows], grad_v.at[rows], in_sems.at[part])
        )
        stores.append(
            pltpu.make_async_copy(grad_v.at[rows], grad_out.at[rows], out_sems.at[part])
        )
    loads.append(pltpu.make_async_copy(probe_hbm, probe_v, in_sems.at[count]))
    stores.append(pltpu.make_async_copy(probe_v, probe_out, out_sems.at[count]))
    for load in loads:
        load.start()
    for load, store in zip(loads, stores):
        load.wait()
        store.start()
    for store in stores:
        store.wait()


def body(
    sizes,
    densities,
    spectra,
    intensities,
    positions,
    probe,
    line_channels,
    line_weights,
    atten_coef,
    beta_coef,
    delta_coef,
):
    n_grp, n_row, n_x, n_zh, total = sizes
    chirps, right, left = constant_tables()
    dens = densities.reshape(E, NB, ZB * X, 128)
    spec = spectra.reshape(ZB * 128, C)
    vmem = pl.BlockSpec(memory_space=pltpu.VMEM)
    smem = pl.BlockSpec(memory_space=pltpu.SMEM)
    anywhere = pl.BlockSpec(memory_space=pl.ANY)
    n_near = n_grp * n_zh
    dma = pltpu.SemaphoreType.DMA
    small = (NB, 3, ZB, 128)
    out, probe_grad = pl.pallas_call(
        functools.partial(kernel, sizes),
        out_shape=(
            jax.ShapeDtypeStruct((E, NB, ZB * X, 128), BF16),
            jax.ShapeDtypeStruct((2, M * M), F32),
        ),
        in_specs=[
            anywhere,
            anywhere,
            anywhere,
            smem,
            vmem,
            vmem,
            vmem,
            smem,
            smem,
            smem,
            vmem,
            vmem,
            vmem,
        ],
        out_specs=(anywhere, vmem),
        scratch_shapes=[
            pltpu.VMEM((E, NB, ZB * X, 128), BF16),
            pltpu.VMEM((E, NB, ZB * X, 128), F32),
            pltpu.VMEM((ZB * 128, C), BF16),
            pltpu.VMEM((K, M * M), BF16),
            pltpu.VMEM((K * M, 128), F32),
            pltpu.VMEM((2, M, 128), F32),
            pltpu.VMEM(small, F32),
            pltpu.VMEM(small, F32),
            pltpu.VMEM((NB, 2, E, 8, 128), F32),
            pltpu.VMEM((NB, 2, E, 8, 128), F32),
            pltpu.VMEM(small, F32),
            pltpu.VMEM(small, F32),
            pltpu.VMEM((NB, X, ZB, 128), F32),
            pltpu.VMEM((NB, 2, ZB, 128), F32),
            pltpu.VMEM((NB, 2, ZB, 128), F32),
            pltpu.VMEM(small, F32),
            pltpu.VMEM(small, F32),
            pltpu.VMEM((NB, 2, E, 8, 128), F32),
            pltpu.VMEM((ZB * E, 128), F32),
            pltpu.VMEM((E, ZB * 128), F32),
            pltpu.VMEM((E, NB, ZB * X, 128), BF16),
            pltpu.VMEM((128, 256), F32),
            pltpu.VMEM((2, M, 128), F32),
            pltpu.VMEM((M, 128), F32),
            pltpu.VMEM((NB, M, 128), F32),
            pltpu.VMEM((n_near, M, 128), F32),
            pltpu.VMEM((n_x, M, 128), F32),
            pltpu.VMEM((M, 128), F32),
            dma((NB,)),
            dma,
            dma,
            dma((NB,)),
            dma((NB,)),
            dma((NB,)),
            dma((NB, 2)),
            dma((NB, 2)),
            dma((NB,)),
            dma((NB,)),
            dma((NB,)),
            dma((NB,)),
            dma((NB,)),
            dma((NB,)),
            dma((14,)),
            dma((NB, 2)),
            dma,
            dma((NB,)),
            dma((n_near,)),
            dma((n_near,)),
            dma((n_x,)),
            dma((n_x,)),
            dma((NB,)),
            dma,
            pltpu.SemaphoreType.REGULAR,
        ],
        compiler_params=pltpu.CompilerParams(
            collective_id=0, has_side_effects=True, vmem_limit_bytes=60 * 1024 * 1024
        ),
    )(
        dens,
        spec,
        intensities,
        positions.T,
        probe,
        line_channels.T,
        line_weights.T,
        atten_coef,
        beta_coef,
        delta_coef,
        jnp.asarray(chirps),
        jnp.asarray(right),
        jnp.asarray(left),
    )
    out, probe_grad = pl.pallas_call(
        hand_over,
        out_shape=(
            jax.ShapeDtypeStruct(out.shape, BF16),
            jax.ShapeDtypeStruct(probe_grad.shape, F32),
        ),
        in_specs=[anywhere, anywhere],
        out_specs=(anywhere, anywhere),
        scratch_shapes=[
            pltpu.VMEM(out.shape, BF16),
            pltpu.VMEM(probe_grad.shape, F32),
            dma((E // PART + 1,)),
            dma((E // PART + 1,)),
        ],
        compiler_params=pltpu.CompilerParams(vmem_limit_bytes=60 * 1024 * 1024),
    )(out, probe_grad)
    return out.reshape(densities.shape), probe_grad


def solution(mesh):
    n_grp, n_beam, n_row = mesh.shape["grp"], mesh.shape["beam"], mesh.shape["row"]
    n_zh = 4 if n_row % 4 == 0 else 1
    sizes = (n_grp, n_row, n_row // n_zh, n_zh, float(K * n_grp * n_beam * n_row))
    return jax.shard_map(
        functools.partial(body, sizes),
        mesh=mesh,
        in_specs=(
            P(None, "grp", "beam", "row"),
            P(("grp", "beam"), "row", None),
            P(("grp", "beam", "row"), None),
            P(("grp", "beam", "row"), None),
            P(),
            P(),
            P(),
            P(),
            P(),
            P(),
        ),
        out_specs=(P(None, "grp", "beam", "row"), P()),
        check_vma=False,
    )
```

```python
import functools
import math

import jax
import jax.numpy as jnp
import numpy as np
from jax import lax
from jax.experimental import pallas as pl
from jax.experimental.pallas import tpu as pltpu
from jax.sharding import PartitionSpec as P

E = 32
C = 512
M = 64
K = 32
X = 4
ZB = 16
NB = 8
GROUP = 16
NEAREST = (4, 1, 7, 3, 5, 2, 6)
ORDER = tuple((step, half) for half in range(2) for step in NEAREST)
EARLY = 7
PART = 4

F32 = jnp.float32
BF16 = jnp.bfloat16
HIGHEST = lax.Precision.HIGHEST
MESH = pl.DeviceIdType.MESH
object_weight = 1000.0


def halves(values):
    high = values.astype(BF16)
    return high, (values - high.astype(F32)).astype(BF16)


def swap(values):
    return pltpu.roll(values, M, 1)


def matmul(left, right):
    return jnp.dot(left, right, preferred_element_type=F32)


def np_halves(values):
    high = values.astype(np.float32).astype(jnp.bfloat16)
    low = (values - high.astype(np.float64)).astype(np.float32).astype(jnp.bfloat16)
    return high, low


def constant_tables():
    index = np.arange(M)
    angles = 2.0 * math.pi / M * (index[:, None] * index[None, :] % M)
    dft_real = np.cos(angles) / math.sqrt(M)
    dft_imag = -np.sin(angles) / math.sqrt(M)
    centred = np.arange(M) - M // 2
    chirp = math.pi * 0.5 / M * (centred[:, None] ** 2 + centred[None, :] ** 2)
    chirp_real, chirp_imag = np.cos(chirp), np.sin(chirp)
    chirps = np.stack(
        [
            np.concatenate([chirp_real, chirp_real], 1),
            np.concatenate([-chirp_imag, chirp_imag], 1),
        ]
    ).astype(np.float32)

    def right_table(sign):
        table = np.block([[dft_real, sign * dft_imag], [-sign * dft_imag, dft_real]])
        high, low = np_halves(table)
        row = np.concatenate([high, low], 1)
        return np.concatenate([row, row], 0)

    right = np.stack([right_table(1.0), right_table(-1.0)])
    high, low = np_halves(np.concatenate([dft_real, dft_imag], 0))
    left = np.concatenate([high, high, low, low], 1)
    return chirps, right, left


def kernel(
    sizes,
    dens_hbm,
    spec_hbm,
    inten_hbm,
    pos_ref,
    probe_ref,
    chan_ref,
    weight_ref,
    atten_ref,
    beta_ref,
    delta_ref,
    chirp_ref,
    right_ref,
    left_ref,
    out_hbm,
    probe_out,
    dens_bf,
    dens_f,
    spec_v,
    inten_bf,
    inten_f,
    image_ref,
    tap_src,
    tap_rcv,
    u_src,
    u_rcv,
    ow_src,
    ow_rcv,
    inc_ref,
    tg_src,
    tg_rcv,
    lg_src,
    lg_rcv,
    eg_ref,
    mix_ref,
    fit_ref,
    out_v,
    tile_ref,
    pgsum_ref,
    pr_src,
    pr_rcv,
    pa_rcv,
    pb_rcv,
    pf_rcv,
    dens_sem,
    spec_sem,
    inten_sem,
    out_sem,
    tap_ss,
    tap_rs,
    u_ss,
    u_rs,
    ow_ss,
    ow_rs,
    tg_ss,
    tg_rs,
    lg_ss,
    lg_rs,
    eg_ss,
    eg_rs,
    pr_ss,
    pr_rs,
    pa_ss,
    pa_rs,
    pb_ss,
    pb_rs,
    pf_ss,
    pf_rs,
    hello_sem,
):
    n_grp, n_row, n_x, n_zh, total = sizes
    me = lax.axis_index("beam")
    grp = lax.axis_index("grp")
    row = lax.axis_index("row")
    row_x, row_z = row // n_zh, row % n_zh
    n_near = n_grp * n_zh
    near = grp * n_zh + row_z

    def near_id(step):
        other = (near + step) % n_near
        return {"grp": other // n_zh, "row": row_x * n_zh + other % n_zh}

    def x_id(step):
        return {"row": ((row_x + step) % n_x) * n_zh + row_z}

    def peer(step):
        return (me + step) % NB

    def remote(source, target, send, recv, device):
        return pltpu.make_async_remote_copy(
            src_ref=source,
            dst_ref=target,
            send_sem=send,
            recv_sem=recv,
            device_id=device,
            device_id_type=MESH,
        )

    barrier = pltpu.get_barrier_semaphore()
    is_lead = me == 0
    for step in range(1, NB):
        dst = peer(step)

        @pl.when(dst != 0)
        def _():
            pl.semaphore_signal(barrier, inc=1, device_id={"beam": dst}, device_id_type=MESH)

    @pl.when(is_lead)
    def _():
        for step in range(1, n_near):
            pl.semaphore_signal(barrier, inc=1, device_id=near_id(step), device_id_type=MESH)
        for step in range(1, n_x):
            pl.semaphore_signal(barrier, inc=1, device_id=x_id(step), device_id_type=MESH)

    def dens_copy(step):
        block = (me + 1 + step) % NB
        return pltpu.make_async_copy(
            dens_hbm.at[:, block], dens_bf.at[:, block], dens_sem.at[step]
        )

    for step in range(NB):
        dens_copy(step).start()
    spec_copy = pltpu.make_async_copy(spec_hbm, spec_v, spec_sem)
    spec_copy.start()
    inten_copy = pltpu.make_async_copy(inten_hbm, inten_bf, inten_sem)
    inten_copy.start()

    def cell(e, block, x):
        return dens_f[e, block, pl.ds(x, ZB, stride=X), :]

    def project(step, carry):
        block = (me + 1 + step) % NB
        dens_copy(step).wait()
        dens_f[:, block] = dens_bf[:, block].astype(F32)

        def add(e, sums):
            cells = [cell(e, block, x) for x in range(X)]
            total_cells = (cells[0] + cells[1]) + (cells[2] + cells[3])
            optical = [sums[x] + atten_ref[e] * cells[x] for x in range(X)]
            return (
                *optical,
                sums[X] + beta_ref[e] * total_cells,
                sums[X + 1] + delta_ref[e] * total_cells,
            )

        zero = jnp.zeros((ZB, 128), F32)
        sums = lax.fori_loop(0, E, add, (zero,) * (X + 2), unroll=E)
        depth = zero
        for x in range(X):
            inc_ref[block, x] = jnp.exp(-depth)
            depth = depth + sums[x]
        tap_src[block, 0] = depth
        tap_src[block, 1] = sums[X]
        tap_src[block, 2] = sums[X + 1]

        return carry

    lax.fori_loop(0, NB, project, 0)
    @pl.when(jnp.logical_not(is_lead))
    def _():
        pl.semaphore_wait(barrier, NB - 1)
        pl.semaphore_signal(hello_sem, inc=1, device_id={"beam": 0}, device_id_type=MESH)

    @pl.when(is_lead)
    def _():
        pl.semaphore_wait(hello_sem, NB - 1)

    tap_sends, u_sends = [], []

    def send_tap(step):
        dst = peer(step)
        copy = remote(
            tap_src.at[dst], tap_rcv.at[me], tap_ss.at[step], tap_rs.at[me], {"beam": dst}
        )
        copy.start()
        tap_sends.append(copy)

    def u_copy(step, half):
        dst = peer(step)
        return remote(
            u_src.at[dst, half],
            u_rcv.at[me, half],
            u_ss.at[step, half],
            u_rs.at[me, half],
            {"beam": dst},
        )

    def send_u(step, half):
        copy = u_copy(step, half)
        copy.start()
        u_sends.append(copy)

    def wait_u(half):
        for step in range(1, NB):
            src = peer(step)
            remote(
                u_src.at[src, half],
                u_rcv.at[src, half],
                u_ss.at[step, half],
                u_rs.at[src, half],
                {"beam": src},
            ).wait_recv()

    for step in range(1, NB):
        send_tap(step)
    tap_rcv[me] = tap_src[me]

    def emit(step, carry):
        block = (me + 1 + step) % NB
        local = [inc_ref[block, x] for x in range(X)]

        def one(e, inner):
            terms = [cell(e, block, x) * local[x] for x in range(1, X)]
            value = (cell(e, block, 0) + terms[0]) + (terms[1] + terms[2])
            u_src[block, 0, e] = value[:8]
            u_src[block, 1, e] = value[8:]
            return inner

        lax.fori_loop(0, E, one, 0, unroll=E)

        return carry

    lax.fori_loop(0, NB, emit, 0)
    for step, half in ORDER[:EARLY]:
        send_u(step, half)
    u_rcv[me] = u_src[me]

    for step in range(1, NB):
        src = peer(step)
        remote(tap_src.at[src], tap_rcv.at[src], tap_ss.at[0], tap_rs.at[src], {"beam": src}).wait_recv()
    before = jnp.zeros((ZB, 128), F32)
    absorb = jnp.zeros((ZB, 128), F32)
    phase = jnp.zeros((ZB, 128), F32)
    for d in range(NB):
        ow_src[d, 2] = jnp.exp(-before)
        before = before + tap_rcv[d, 0]
        absorb = absorb + tap_rcv[d, 1]
        phase = phase + tap_rcv[d, 2]
    amplitude = jnp.exp(-absorb)
    own_real = amplitude * jnp.cos(phase)
    own_imag = amplitude * jnp.sin(phase)
    for d in range(NB):
        ow_src[d, 0] = own_real
        ow_src[d, 1] = own_imag
    ow_sends = []
    for step in range(1, NB):
        dst = peer(step)
        copy = remote(
            ow_src.at[dst], ow_rcv.at[me], ow_ss.at[step], ow_rs.at[me], {"beam": dst}
        )
        copy.start()
        ow_sends.append(copy)
    ow_rcv[me] = ow_src[me]
    for step, half in ORDER[EARLY:]:
        send_u(step, half)

    eye = (
        lax.broadcasted_iota(jnp.int32, (E, E), 0) == lax.broadcasted_iota(jnp.int32, (E, E), 1)
    ).astype(F32)

    def columns_of(rows):
        return lax.dot_general(
            eye, rows, (((1,), (1,)), ((), ())), precision=HIGHEST, preferred_element_type=F32
        )

    lines = columns_of(chan_ref[...].astype(F32))
    strengths = columns_of(weight_ref[...])
    channel = lax.broadcasted_iota(jnp.int32, (E, C), 1).astype(F32)
    table = jnp.zeros((E, C), F32)
    for line in range(4):
        offset = channel - lines[:, line : line + 1]
        table = table + strengths[:, line : line + 1] * jnp.exp(-offset * offset / 8.0)
    gram = lax.dot_general(
        table, table, (((1,), (1,)), ((), ())), precision=HIGHEST, preferred_element_type=F32
    )
    gram_high, gram_low = halves(gram)
    gram_parts = jnp.concatenate([gram_high, gram_low], 0)

    spec_copy.wait()
    table_high, table_low = halves(table)
    fit = lax.dot_general(
        jnp.concatenate([table_high, table_low], 0),
        spec_v[...],
        (((1,), (1,)), ((), ())),
        preferred_element_type=F32,
    )
    fit_ref[...] = fit[:E] + fit[E:]

    lane = lax.broadcasted_iota(jnp.int32, (M, 128), 1)
    first = lane < M
    even = lax.broadcasted_iota(jnp.int32, (M, 128), 0) % 2 == 0
    inten_copy.wait()
    flat = inten_bf[...].astype(F32)
    for g in range(M // 2):
        group = flat[:, g * 128 : (g + 1) * 128]
        inten_f[pl.ds(2 * g, K, stride=M), :] = group
        inten_f[pl.ds(2 * g + 1, K, stride=M), :] = group
    for part in range(2):
        for g in range(M // 2):
            group = probe_ref[part : part + 1, g * 128 : (g + 1) * 128]
            image_ref[part, 2 * g : 2 * g + 1, :] = group
            image_ref[part, 2 * g + 1 : 2 * g + 2, :] = group
    image_real, image_imag = image_ref[0], image_ref[1]
    probe = jnp.where(
        first,
        jnp.where(even, image_real, swap(image_real)),
        jnp.where(even, swap(image_imag), image_imag),
    )
    keep = first == even

    for step in range(1, NB):
        src = peer(step)
        remote(ow_src.at[src], ow_rcv.at[src], ow_ss.at[0], ow_rs.at[src], {"beam": src}).wait_recv()

    illum = probe * chirp_ref[0] + swap(probe) * chirp_ref[1]
    illum_swap = swap(illum)
    illum_a = jnp.where(first, illum, illum_swap)
    illum_b = jnp.where(first, -illum_swap, illum)
    sign = jnp.where(first, -1.0, 1.0).astype(F32)

    obj_real = ow_rcv[:, 0].reshape(NB * ZB, 128)
    obj_imag = ow_rcv[:, 1].reshape(NB * ZB, 128)
    real_high, real_low = halves(obj_real)
    imag_high, imag_low = halves(obj_imag)
    field = jnp.concatenate([real_high, imag_high, real_low, imag_low], 1)

    pick_z = lax.broadcasted_iota(jnp.int32, (M, 128), 1) - lax.broadcasted_iota(
        jnp.int32, (M, 128), 0
    )
    gather_row = lax.broadcasted_iota(jnp.int32, (256, 128), 0)
    gather_col = lax.broadcasted_iota(jnp.int32, (256, 128), 1)
    pick_y = jnp.where(
        (gather_row < 128) == (gather_col < M), gather_row % 128 - gather_col % M, -1
    )
    spread_row = lax.broadcasted_iota(jnp.int32, (128, 256), 0)
    spread_col = lax.broadcasted_iota(jnp.int32, (128, 256), 1)
    place_y = jnp.where(
        (spread_col < 128) == (spread_row < M), spread_col % 128 - spread_row % M, -1
    )
    place_z = lax.broadcasted_iota(jnp.int32, (128, 128), 0) - (
        lax.broadcasted_iota(jnp.int32, (128, 128), 1) % M
    )

    tile_ref[...] = jnp.zeros(tile_ref.shape, F32)
    pgsum_ref[...] = jnp.zeros(pgsum_ref.shape, F32)

    def transform(values, right, conj):
        high, low = halves(values)
        product = matmul(jnp.concatenate([high, low], 1), right)
        product = product[:, :128] + product[:, 128:]
        high, low = halves(product)
        outs = []
        for i in range(GROUP):
            part = slice(i * M, (i + 1) * M)
            stack = jnp.concatenate([high[part], low[part], high[part], low[part]], 0)
            both = matmul(left_ref[...], stack)
            turned = swap(both[M:]) * sign
            outs.append(both[:M] - turned if conj else both[:M] + turned)
        return outs

    def positions_step(group, carry):
        windows, picks = [], []
        starts = [
            (pos_ref[0, group * GROUP + i], pos_ref[1, group * GROUP + i])
            for i in range(GROUP)
        ]
        for i in range(GROUP):
            rows = (pick_z == starts[i][0]).astype(F32).astype(BF16)
            cut = matmul(rows, field).astype(BF16)
            stack = jnp.concatenate([cut[:, :256], cut[:, 256:]], 0)
            columns = (pick_y == starts[i][1]).astype(F32).astype(BF16)
            both = matmul(stack, columns)
            windows.append(both[:M] + both[M:])
        exits = [w * illum_a + swap(w) * illum_b for w in windows]
        far = transform(jnp.concatenate(exits, 0), right_ref[0], False)
        pulled = []
        for i in range(GROUP):
            square = far[i] * far[i]
            start = pl.multiple_of((group * GROUP + i) * M, M)
            measured = inten_f[pl.ds(start, M), :]
            measured = jnp.where(keep, measured, swap(measured))
            misfit = square + swap(square) - measured
            pulled.append(misfit * far[i])
        back = transform(jnp.concatenate(pulled, 0), right_ref[1], True)
        sum_a = pgsum_ref[0]
        sum_b = pgsum_ref[1]
        tile = tile_ref[...]
        for i in range(GROUP):
            sum_a = sum_a + windows[i] * back[i]
            sum_b = sum_b + swap(windows[i]) * back[i]
            grad = back[i] * illum_a - swap(back[i]) * illum_b
            high, low = halves(grad)
            columns = (place_y == starts[i][1]).astype(F32).astype(BF16)
            spread = matmul(jnp.concatenate([high, low], 0), columns).astype(BF16)
            rows = (place_z == starts[i][0]).astype(F32).astype(BF16)
            tile = tile + matmul(rows, spread)
        pgsum_ref[0] = sum_a
        pgsum_ref[1] = sum_b
        tile_ref[...] = tile
        return carry

    lax.fori_loop(0, K // GROUP, positions_step, 0)

    for d in range(NB):
        tg_src[d, 0] = tile_ref[d * ZB : (d + 1) * ZB, :128]
        tg_src[d, 1] = tile_ref[d * ZB : (d + 1) * ZB, 128:]
    sum_a, sum_b = pgsum_ref[0], pgsum_ref[1]
    conj_sum = jnp.where(first, sum_a + swap(sum_a), sum_b - swap(sum_b))
    local_probe = conj_sum * chirp_ref[0] - swap(conj_sum) * chirp_ref[1]
    image_ref[0] = local_probe
    upper, lower = image_ref[0, pl.ds(0, M // 2, stride=2), :], image_ref[0, pl.ds(1, M // 2, stride=2), :]
    half_first = first[: M // 2]
    flat_real = jnp.where(half_first, upper, swap(lower))
    flat_imag = jnp.where(half_first, swap(upper), lower)
    pr_src[: M // 2] = flat_real
    pr_src[M // 2 :] = flat_imag
    tg_sends = []
    for step in range(1, NB):
        dst = peer(step)
        copy = remote(
            tg_src.at[dst], tg_rcv.at[me], tg_ss.at[step], tg_rs.at[me], {"beam": dst}
        )
        copy.start()
        tg_sends.append(copy)

    def pr_copy(src):
        return remote(pr_src, pr_rcv.at[src], pr_ss, pr_rs.at[src], {"beam": 0})

    @pl.when(jnp.logical_not(is_lead))
    def _():
        pr_copy(me).start()

    tg_rcv[me] = tg_src[me]

    def scale_block(block, carry):
        for x in range(X):
            inc_ref[block, x] = inc_ref[block, x] * ow_rcv[block, 2]
        return carry

    lax.fori_loop(0, NB, scale_block, 0)

    shield = [ow_src[d, 2] for d in range(NB)]

    def own_half(half):
        rows = slice(half * 8, half * 8 + 8)
        count = E * 8

        def add_slabs(e, carry):
            value = u_rcv[0, half, e] * shield[0][rows]
            for d in range(1, NB):
                value = value + u_rcv[d, half, e] * shield[d][rows]
            mix_ref[pl.ds(half * count + e, 8, stride=E), :] = value
            return carry

        lax.fori_loop(0, E, add_slabs, 0, unroll=E)
        columns = jnp.concatenate(
            [mix_ref[half * count + z * E : half * count + (z + 1) * E, :] for z in range(8)], 1
        )
        high, low = halves(columns)
        product = matmul(gram_parts, jnp.concatenate([high, low], 1))
        product = product[:E] + product[E:]
        grads = (product[:, :1024] + product[:, 1024:]) - fit_ref[:, half * 1024 : half * 1024 + 1024]
        for z in range(8):
            mix_ref[half * count + z * E : half * count + (z + 1) * E, :] = grads[
                :, z * 128 : (z + 1) * 128
            ]

        def to_layers(e, carry):
            eg_ref[me, half, e] = mix_ref[pl.ds(half * count + e, 8, stride=E), :]
            return carry

        lax.fori_loop(0, E, to_layers, 0, unroll=E)

    beam_z, beam_y = me // 4, me % 4
    up = beam_z * 4 + (beam_y + 1) % 4
    down = beam_z * 4 + (beam_y + 3) % 4
    across = (1 - beam_z) * 4 + beam_y
    far_side = beam_z * 4 + (beam_y + 2) % 4
    across_up = (1 - beam_z) * 4 + (beam_y + 1) % 4
    across_down = (1 - beam_z) * 4 + (beam_y + 3) % 4
    across_far = (1 - beam_z) * 4 + (beam_y + 2) % 4

    eg_sends = []

    def hand(block, half, dst):
        copy = remote(
            eg_ref.at[block, half],
            eg_ref.at[block, half],
            eg_ss.at[len(eg_sends)],
            eg_rs.at[block, half],
            {"beam": dst},
        )
        copy.start()
        eg_sends.append(copy)

    def arrive(block, half):
        remote(
            eg_ref.at[block, half],
            eg_ref.at[block, half],
            eg_ss.at[0],
            eg_rs.at[block, half],
            {"beam": block},
        ).wait_recv()

    wait_u(0)
    own_half(0)
    hand(me, 0, up)
    hand(me, 0, across)
    hand(me, 0, down)
    wait_u(1)

    def pa_copy(step, owner):
        return remote(
            pa_rcv.at[owner], pa_rcv.at[owner], pa_ss.at[step], pa_rs.at[owner], near_id(step)
        )

    def pb_copy(step, owner):
        return remote(
            pb_rcv.at[owner], pb_rcv.at[owner], pb_ss.at[step], pb_rs.at[owner], x_id(step)
        )

    def pf_copy(step):
        return remote(pf_rcv, pf_rcv, pf_ss.at[step], pf_rs, {"beam": peer(step)})

    @pl.when(is_lead)
    def _():
        for src in range(1, NB):
            pr_copy(src).wait_recv()
        piece = pr_src[...]
        for src in range(1, NB):
            piece = piece + pr_rcv[src]
        pa_rcv[near] = piece
        pl.semaphore_wait(barrier, n_near - 1 + n_x - 1)
        for step in range(1, n_near):
            pa_copy(step, near).start()

    own_half(1)

    def weigh(e, sums):
        value = jnp.concatenate([eg_ref[me, 0, e], eg_ref[me, 1, e]], 0)
        return tuple(
            sums[d] + value * jnp.concatenate([u_rcv[d, 0, e], u_rcv[d, 1, e]], 0)
            for d in range(NB)
        )

    weighted = lax.fori_loop(0, E, weigh, (jnp.zeros((ZB, 128), F32),) * NB, unroll=8)

    for step in range(1, NB):
        src = peer(step)
        remote(tg_src.at[src], tg_rcv.at[src], tg_ss.at[0], tg_rs.at[src], {"beam": src}).wait_recv()
    tile_real = tg_rcv[0, 0]
    tile_imag = tg_rcv[0, 1]
    for d in range(1, NB):
        tile_real = tile_real + tg_rcv[d, 0]
        tile_imag = tile_imag + tg_rcv[d, 1]
    own_real, own_imag = ow_src[0, 0], ow_src[0, 1]
    grad_absorb = -object_weight * (own_real * tile_real + own_imag * tile_imag)
    grad_phase = object_weight * (own_real * tile_imag - own_imag * tile_real)
    later = jnp.zeros((ZB, 128), F32)
    for d in range(NB - 1, -1, -1):
        lg_src[d, 0] = later
        lg_src[d, 1] = grad_absorb
        lg_src[d, 2] = grad_phase
        later = later + weighted[d] * shield[d]
    lg_sends = []
    for step in range(1, NB):
        dst = peer(step)
        copy = remote(
            lg_src.at[dst], lg_rcv.at[me], lg_ss.at[step], lg_rs.at[me], {"beam": dst}
        )
        copy.start()
        lg_sends.append(copy)
    lg_rcv[me] = lg_src[me]

    hand(me, 1, down)
    hand(me, 1, across)
    hand(me, 1, up)

    def out_copy(order, block):
        return pltpu.make_async_copy(
            out_v.at[:, block], out_hbm.at[:, block], out_sem.at[order]
        )

    def finish(order, block):
        def grad_of(e):
            return jnp.concatenate([eg_ref[block, 0, e], eg_ref[block, 1, e]], 0)

        def weigh_cells(e, sums):
            value = grad_of(e)
            return tuple(sums[x] + value * cell(e, block, x) for x in range(X))

        zero = jnp.zeros((ZB, 128), F32)
        sums = lax.fori_loop(0, E, weigh_cells, (zero,) * X, unroll=E)
        light = [inc_ref[block, x] for x in range(X)]
        beyond = [None] * X
        running = lg_rcv[block, 0]
        for x in range(X - 1, -1, -1):
            beyond[x] = running
            running = running + light[x] * sums[x]
        absorb_grad, phase_grad = lg_rcv[block, 1], lg_rcv[block, 2]

        def write(e, carry):
            value = grad_of(e)
            shared = beta_ref[e] * absorb_grad + delta_ref[e] * phase_grad
            for x in range(X):
                result = value * light[x] - atten_ref[e] * beyond[x] + shared
                dens_f[e, block, pl.ds(x, ZB, stride=X), :] = result
            out_v[e, block] = dens_f[e, block].astype(BF16)
            return carry

        lax.fori_loop(0, E, write, 0, unroll=E)
        out_copy(order, block).start()

    def extras(block):
        remote(lg_src.at[block], lg_rcv.at[block], lg_ss.at[0], lg_rs.at[block], {"beam": block}).wait_recv()

    arrive(down, 0)
    hand(down, 0, up)
    arrive(across, 0)
    hand(across, 0, up)
    hand(across, 0, down)
    arrive(up, 1)
    hand(up, 1, down)
    arrive(across, 1)
    hand(across, 1, up)
    hand(across, 1, down)
    finish(0, me)

    @pl.when(is_lead)
    def _():
        for step in range(1, n_near):
            pa_copy(step, (near + step) % n_near).wait_recv()
        piece = pa_rcv[0]
        for d in range(1, n_near):
            piece = piece + pa_rcv[d]
        pb_rcv[row_x] = piece
        for step in range(1, n_x):
            pb_copy(step, row_x).start()

    arrive(down, 1)
    extras(down)
    finish(1, down)
    arrive(far_side, 0)
    hand(far_side, 0, across)
    arrive(far_side, 1)
    hand(far_side, 1, across)

    arrive(up, 0)
    extras(up)
    finish(2, up)
    extras(across)
    finish(3, across)

    extras(far_side)
    finish(4, far_side)

    @pl.when(is_lead)
    def _():
        for step in range(1, n_x):
            pb_copy(step, (row_x + step) % n_x).wait_recv()
        piece = pb_rcv[0]
        for d in range(1, n_x):
            piece = piece + pb_rcv[d]
        pf_rcv[...] = piece * (1.0 / total)
        for step in range(1, NB):
            pf_copy(step).start()

    arrive(across_up, 0)
    arrive(across_up, 1)
    extras(across_up)
    finish(5, across_up)
    arrive(across_down, 0)
    arrive(across_down, 1)
    extras(across_down)
    finish(6, across_down)

    arrive(across_far, 0)
    arrive(across_far, 1)
    extras(across_far)
    finish(7, across_far)

    @pl.when(jnp.logical_not(is_lead))
    def _():
        pf_copy(1).wait_recv()

    for part in range(2):
        for g in range(M // 2):
            row_at = part * (M // 2) + g
            probe_out[part : part + 1, g * 128 : (g + 1) * 128] = pf_rcv[row_at : row_at + 1, :]

    for copy in tap_sends + u_sends + ow_sends + tg_sends + eg_sends + lg_sends:
        copy.wait_send()

    @pl.when(jnp.logical_not(is_lead))
    def _():
        pr_copy(me).wait_send()

    @pl.when(is_lead)
    def _():
        for step in range(1, n_near):
            pa_copy(step, near).wait_send()
        for step in range(1, n_x):
            pb_copy(step, row_x).wait_send()
        for step in range(1, NB):
            pf_copy(step).wait_send()

    for order, block in enumerate(
        [me, down, up, across, far_side, across_up, across_down, across_far]
    ):
        out_copy(order, block).wait()


def hand_over(grad_hbm, probe_hbm, grad_out, probe_out, grad_v, probe_v, in_sems, out_sems):
    count = E // PART
    loads, stores = [], []
    for part in range(count):
        rows = pl.ds(part * PART, PART)
        loads.append(
            pltpu.make_async_copy(grad_hbm.at[rows], grad_v.at[rows], in_sems.at[part])
        )
        stores.append(
            pltpu.make_async_copy(grad_v.at[rows], grad_out.at[rows], out_sems.at[part])
        )
    loads.append(pltpu.make_async_copy(probe_hbm, probe_v, in_sems.at[count]))
    stores.append(pltpu.make_async_copy(probe_v, probe_out, out_sems.at[count]))
    for load in loads:
        load.start()
    for load, store in zip(loads, stores):
        load.wait()
        store.start()
    for store in stores:
        store.wait()


def body(
    sizes,
    densities,
    spectra,
    intensities,
    positions,
    probe,
    line_channels,
    line_weights,
    atten_coef,
    beta_coef,
    delta_coef,
):
    n_grp, n_row, n_x, n_zh, total = sizes
    chirps, right, left = constant_tables()
    dens = densities.reshape(E, NB, ZB * X, 128)
    spec = spectra.reshape(ZB * 128, C)
    vmem = pl.BlockSpec(memory_space=pltpu.VMEM)
    smem = pl.BlockSpec(memory_space=pltpu.SMEM)
    anywhere = pl.BlockSpec(memory_space=pl.ANY)
    n_near = n_grp * n_zh
    dma = pltpu.SemaphoreType.DMA
    small = (NB, 3, ZB, 128)
    out, probe_grad = pl.pallas_call(
        functools.partial(kernel, sizes),
        out_shape=(
            jax.ShapeDtypeStruct((E, NB, ZB * X, 128), BF16),
            jax.ShapeDtypeStruct((2, M * M), F32),
        ),
        in_specs=[
            anywhere,
            anywhere,
            anywhere,
            smem,
            vmem,
            vmem,
            vmem,
            smem,
            smem,
            smem,
            vmem,
            vmem,
            vmem,
        ],
        out_specs=(anywhere, vmem),
        scratch_shapes=[
            pltpu.VMEM((E, NB, ZB * X, 128), BF16),
            pltpu.VMEM((E, NB, ZB * X, 128), F32),
            pltpu.VMEM((ZB * 128, C), BF16),
            pltpu.VMEM((K, M * M), BF16),
            pltpu.VMEM((K * M, 128), F32),
            pltpu.VMEM((2, M, 128), F32),
            pltpu.VMEM(small, F32),
            pltpu.VMEM(small, F32),
            pltpu.VMEM((NB, 2, E, 8, 128), F32),
            pltpu.VMEM((NB, 2, E, 8, 128), F32),
            pltpu.VMEM(small, F32),
            pltpu.VMEM(small, F32),
            pltpu.VMEM((NB, X, ZB, 128), F32),
            pltpu.VMEM((NB, 2, ZB, 128), F32),
            pltpu.VMEM((NB, 2, ZB, 128), F32),
            pltpu.VMEM(small, F32),
            pltpu.VMEM(small, F32),
            pltpu.VMEM((NB, 2, E, 8, 128), F32),
            pltpu.VMEM((ZB * E, 128), F32),
            pltpu.VMEM((E, ZB * 128), F32),
            pltpu.VMEM((E, NB, ZB * X, 128), BF16),
            pltpu.VMEM((128, 256), F32),
            pltpu.VMEM((2, M, 128), F32),
            pltpu.VMEM((M, 128), F32),
            pltpu.VMEM((NB, M, 128), F32),
            pltpu.VMEM((n_near, M, 128), F32),
            pltpu.VMEM((n_x, M, 128), F32),
            pltpu.VMEM((M, 128), F32),
            dma((NB,)),
            dma,
            dma,
            dma((NB,)),
            dma((NB,)),
            dma((NB,)),
            dma((NB, 2)),
            dma((NB, 2)),
            dma((NB,)),
            dma((NB,)),
            dma((NB,)),
            dma((NB,)),
            dma((NB,)),
            dma((NB,)),
            dma((14,)),
            dma((NB, 2)),
            dma,
            dma((NB,)),
            dma((n_near,)),
            dma((n_near,)),
            dma((n_x,)),
            dma((n_x,)),
            dma((NB,)),
            dma,
            pltpu.SemaphoreType.REGULAR,
        ],
        compiler_params=pltpu.CompilerParams(
            collective_id=0, has_side_effects=True, vmem_limit_bytes=60 * 1024 * 1024
        ),
    )(
        dens,
        spec,
        intensities,
        positions.T,
        probe,
        line_channels.T,
        line_weights.T,
        atten_coef,
        beta_coef,
        delta_coef,
        jnp.asarray(chirps),
        jnp.asarray(right),
        jnp.asarray(left),
    )
    out, probe_grad = pl.pallas_call(
        hand_over,
        out_shape=(
            jax.ShapeDtypeStruct(out.shape, BF16),
            jax.ShapeDtypeStruct(probe_grad.shape, F32),
        ),
        in_specs=[anywhere, anywhere],
        out_specs=(anywhere, anywhere),
        scratch_shapes=[
            pltpu.VMEM(out.shape, BF16),
            pltpu.VMEM(probe_grad.shape, F32),
            dma((E // PART + 1,)),
            dma((E // PART + 1,)),
        ],
        compiler_params=pltpu.CompilerParams(vmem_limit_bytes=60 * 1024 * 1024),
    )(out, probe_grad)
    return out.reshape(densities.shape), probe_grad


def solution(mesh):
    n_grp, n_beam, n_row = mesh.shape["grp"], mesh.shape["beam"], mesh.shape["row"]
    n_zh = 4 if n_row % 4 == 0 else 1
    sizes = (n_grp, n_row, n_row // n_zh, n_zh, float(K * n_grp * n_beam * n_row))
    return jax.shard_map(
        functools.partial(body, sizes),
        mesh=mesh,
        in_specs=(
            P(None, "grp", "beam", "row"),
            P(("grp", "beam"), "row", None),
            P(("grp", "beam", "row"), None),
            P(("grp", "beam", "row"), None),
            P(),
            P(),
            P(),
            P(),
            P(),
            P(),
        ),
        out_specs=(P(None, "grp", "beam", "row"), P()),
        check_vma=False,
    )
```
